256 devices in a mesh: orb: 4 (over z_lo, core), dom: 64 (over z_hi, y, x).
Axes of the slice: x: 4, y: 4, z: 8 (z_hi: 4, z_lo: 2; z = z_hi * 2 + z_lo), core: 2. Of those that a mesh axis runs over, the one named last changes fastest.
Arguments:
- orbitals: float32 [2, 16, 256, 64, 128], P(None, 'orb', 'dom'), may hold values from -6 to 6
- occupations: int32 [16], P('orb'), may hold values from 1 to 2
- external: float32 [256, 64, 128], P('dom'), may hold values from -2 to 0.5
- control: float32 [2], replicated, may hold values from -2 to 2
Outputs:
- propagated: float32 [2, 16, 256, 64, 128], P(None, 'orb', 'dom')
- hartree: float32 [256, 64, 128], P('dom')
The draws below stay inside these ranges and needn't reach their ends.
All inputs are finite; a program needn't handle non-finite values.
Results may differ from the reference program's by a relative error of at most 0.00016.
Values sent between devices are 32-bit elements; how exact they have to be, the bound alone decides.
A program may use at most 64 MiB of HBM per device.

```python
import jax
import jax.numpy as jnp
from jax import lax

NORB = 16
NY = 64
NZ = 128
NX = 256
STEPS = 2
TERMS = 4
LEVELS = 3
CYCLES = 2
SWEEPS = 2
COARSE = 4


def draw_orbitals(key, part):
    key = jax.random.fold_in(key, 17)
    place_key, value_key = jax.random.split(key)
    begin = jax.random.randint(place_key, (), NX // 8, 3 * NX // 8 + 1)
    planes = jnp.arange(NX, dtype=jnp.int32)
    inside = (planes >= begin) & (planes < begin + NX // 2)
    shape = (2, NORB, NX, NY, NZ)
    values = jax.random.normal(value_key, shape, jnp.float32)
    scale = jnp.where(inside, 2.2, 0.25)
    return jnp.clip(values * scale[None, None, :, None, None], -6.0, 6.0).astype(jnp.float32)


def with_ends(array, rng, low, top_value):
    shape = array.shape
    spot = [jax.random.randint(jax.random.fold_in(rng, axis), (), 0, shape[axis]) for axis in range(len(shape))]
    array = array.at[tuple(spot)].set(low)
    longest = shape.index(max(shape))
    spot[longest] = (spot[longest] + 1) % shape[longest]
    return array.at[tuple(spot)].set(top_value)


def shard_levels(rng, shape, cuts, low, top_value):
    def one(dim, blocks):
        heights = jax.random.uniform(jax.random.fold_in(jax.random.fold_in(rng, 6), dim), (blocks,), jnp.float32, low / len(cuts), top_value / len(cuts))
        return jnp.repeat(jnp.exp(heights), shape[dim] // blocks).reshape((-1,) + (1,) * (len(shape) - dim - 1))

    level = one(*cuts[0])
    for cut in cuts[1:]:
        level = level * one(*cut)
    return level


def setup_inputs(seed: int = 0) -> dict:
    splits = jax.random.split(jax.random.key(seed), 5)
    return {
        "orbitals": draw_orbitals(jax.random.fold_in(splits[4], 71), 0),
        "occupations": with_ends(jax.random.randint(splits[1], (NORB,), 1, 3), jax.random.fold_in(splits[1], 1), 1, 2).astype(jnp.int32),
        "external": jnp.clip(-2.0 + 2.5 * jax.random.uniform(splits[2], (NX, NY, NZ), jnp.float32) ** shard_levels(splits[2], (NX, NY, NZ), ((0, 64),), -0.2, 0.2), -2.0, 0.5),
        "control": jnp.clip(jax.random.uniform(splits[3], (STEPS,), jnp.float32, -2.0, 2.0), -2.0, 2.0),
    }


time_step = 0.2
omega = 0.8
coupling = 0.025


def neighbour(field, offset, axis):
    count = field.shape[axis]
    reach = abs(offset)
    widths = [(0, 0)] * field.ndim
    widths[axis] = (reach, reach)
    padded = jnp.pad(field, widths)
    return lax.slice_in_dim(padded, reach + offset, reach + offset + count, axis=axis)


def laplace_four(field):
    total = -7.5 * field
    for axis in range(3):
        near = neighbour(field, 1, axis) + neighbour(field, -1, axis)
        far = neighbour(field, 2, axis) + neighbour(field, -2, axis)
        total = total + (4.0 / 3.0) * near - (1.0 / 12.0) * far
    return total


def apply_ham(field, potential):
    return -0.5 * laplace_four(field) + potential * field


def seven(field, level):
    beside = jnp.zeros_like(field)
    for axis in range(3):
        beside = beside + neighbour(field, 1, axis) + neighbour(field, -1, axis)
    return (6.0 * field - beside) / (4.0 ** level)


def restrict(field):
    a, b, c = field.shape
    return field.reshape(a // 2, 2, b // 2, 2, c // 2, 2).mean(axis=(1, 3, 5))


def prolong(field):
    return jnp.repeat(jnp.repeat(jnp.repeat(field, 2, 0), 2, 1), 2, 2)


def vcycle(field, source, level):
    relax = omega * (4.0 ** level) / 6.0
    if level == LEVELS - 1:
        for sweep in range(COARSE):
            field = field + relax * (source - seven(field, level))
        return field
    for sweep in range(SWEEPS):
        field = field + relax * (source - seven(field, level))
    coarse = restrict(source - seven(field, level))
    field = field + prolong(vcycle(jnp.zeros_like(coarse), coarse, level + 1))
    for sweep in range(SWEEPS):
        field = field + relax * (source - seven(field, level))
    return field


def propagate(pair, potential):
    real_part, imag_part = pair
    term_re, term_im = real_part, imag_part
    total_re, total_im = real_part, imag_part
    for order in range(1, TERMS + 1):
        factor = time_step / order
        image_re = apply_ham(term_re, potential)
        image_im = apply_ham(term_im, potential)
        term_re, term_im = factor * image_im, -factor * image_re
        total_re = total_re + term_re
        total_im = total_im + term_im
    return total_re, total_im


def reference(orbitals, occupations, external, control):
    positions = (jnp.arange(NX, dtype=jnp.float32) + 0.5) * (2.0 / NX) - 1.0
    dipole = positions[:, None, None]
    weights = occupations.astype(jnp.float32) / NORB
    real_part, imag_part = orbitals[0], orbitals[1]
    hartree = jnp.zeros((NX, NY, NZ), jnp.float32)
    for step in range(STEPS):
        def add_orbital(total, item):
            weight, re_one, im_one = item
            return total + weight * (re_one * re_one + im_one * im_one), None
        density, unused = lax.scan(add_orbital, jnp.zeros((NX, NY, NZ), jnp.float32), (weights, real_part, imag_part))
        source = coupling * density
        hartree = jnp.zeros_like(source)
        for cycle in range(CYCLES):
            hartree = vcycle(hartree, source, 0)
        potential = external + hartree + control[step] * dipole
        real_part, imag_part = lax.map(lambda pair: propagate(pair, potential), (real_part, imag_part))
    return jnp.stack([real_part, imag_part]), hartree
```

```python
import functools

import jax
import jax.numpy as jnp
from jax import lax
from jax.experimental import pallas as pl
from jax.experimental.pallas import tpu as pltpu
from jax.sharding import PartitionSpec as P

STEPS = 2
TERMS = 4
TIME_STEP = 0.2
COUPLING = 0.025
RELAX = 0.8 / 6.0
KEEP = 0.2

ORB = 4
DOM = 64
RING = 4
GROUPS = DOM // RING
SLAB = 4
GROUP = RING * SLAB
WIDE = 8
NX = DOM * SLAB
NY, NZ = 64, 128
EXT = GROUP + 2 * WIDE
FEXT = SLAB + 2 * WIDE
REACH = 7
SLABS = 2 * REACH + 1
Y1, Y2 = NY // 2, NY // 4
COPIES = 160
HIGH = lax.Precision.HIGHEST


def dot(a, b):
    return jnp.dot(a, b, precision=HIGH, preferred_element_type=jnp.float32)


def iota(shape, dim):
    return lax.broadcasted_iota(jnp.int32, shape, dim)


def shifted(u, reach, axis, first, last):
    size = u.shape[axis]
    place = iota(u.shape, axis)
    low = jnp.where(place >= first + reach, pltpu.roll(u, reach, axis), 0.0)
    high = jnp.where(place <= last - reach, pltpu.roll(u, size - reach, axis), 0.0)
    return low + high


def plane_pair(u, reach):
    return shifted(u, reach, 0, 0, NY - 1) + shifted(u, reach, 1, 0, NZ - 1)


def beside_fine(ref, p):
    u = ref[p]
    return u, ref[p - 1] + ref[p + 1] + plane_pair(u, 1)


def beside_mid(ref):
    u = ref[1 : SLABS + 1]
    lane = iota(u.shape, 2)
    inner = lane % 64
    across = jnp.where(lane < 64, ref[2 : SLABS + 2], ref[0:SLABS])
    total = pltpu.roll(u + across, 64, 2)
    total = total + shifted(u, 1, 1, 0, Y1 - 1)
    total = total + jnp.where(inner >= 1, pltpu.roll(u, 1, 2), 0.0)
    total = total + jnp.where(inner <= 62, pltpu.roll(u, 127, 2), 0.0)
    return u, total


def beside_low(ref):
    u = ref[1 : SLABS + 1]
    total = ref[2 : SLABS + 2] + ref[0:SLABS]
    total = total + shifted(u, 1, 1, 0, Y2 - 1) + shifted(u, 1, 2, 0, 31)
    return u, total


def kernel(
    psi_in, occ, ext, control, psi_out, hartree_out,
    psi, t1, t2, t3, pot, part, ringpart, half, d1, d2, f, va, vb, c1, m_a, m_b, l_a, l_b, mask1, mask2,
    tmp_res, tmp_mid, tmp_low, up, send, recv, local_sem,
):
    o = lax.axis_index("orb")
    d = lax.axis_index("dom")
    x = lax.rem(d, RING)
    g = lax.div(d, RING)

    barrier = pltpu.get_barrier_semaphore()
    for k in range(1, REACH + 1):
        for to in (lax.rem(d + k, DOM), lax.rem(d + DOM - k, DOM)):
            pl.semaphore_signal(barrier, inc=1, device_id={"orb": o, "dom": to})
    for k in range(1, ORB):
        pl.semaphore_signal(barrier, inc=1, device_id={"orb": lax.rem(o + k, ORB), "dom": d})

    own = pltpu.make_async_copy(
        psi_in.at[:, x], psi.at[0, :, pl.ds(WIDE + SLAB * x, SLAB)], local_sem.at[0]
    )
    own.start()

    def weight(b):
        return occ[b].astype(jnp.float32) * (1.0 / 16.0)

    for p in range(SLAB):
        total = jnp.zeros((NY, NZ), jnp.float32)
        for b in range(4):
            re, im = psi_in[0, b, p], psi_in[1, b, p]
            total = total + weight(b) * (re * re + im * im)
        part[0, p] = total

    for s in range(SLABS):
        inside = jnp.logical_and(d - REACH + s >= 0, d - REACH + s < DOM)
        factor = jnp.where(inside, 1.0, 0.0).astype(jnp.float32)
        mask1[s] = jnp.full((Y1, NZ), 1.0, jnp.float32) * factor
        mask2[s] = jnp.full((Y2, NZ), 1.0, jnp.float32) * factor
    for ref in (m_a, m_b, l_a, l_b):
        ref[0] = jnp.zeros(ref.shape[1:], jnp.float32)
        ref[SLABS + 1] = jnp.zeros(ref.shape[1:], jnp.float32)

    def clear_fine(p, carry):
        va[p] = jnp.zeros((NY, NZ), jnp.float32)
        vb[p] = jnp.zeros((NY, NZ), jnp.float32)
        return carry

    lax.fori_loop(0, FEXT, clear_fine, 0)

    def clear_halo(begin, refs):
        def body(p, carry):
            for ref in refs:
                for c in range(2):
                    ref[c, p] = jnp.zeros((NY, NZ), jnp.float32)
            return carry

        lax.fori_loop(begin, begin + WIDE, body, 0)

    @pl.when(g == 0)
    def _():
        clear_halo(0, (t1, t2, t3))

    @pl.when(g == GROUPS - 1)
    def _():
        clear_halo(WIDE + GROUP, (t1, t2, t3))

    pl.semaphore_wait(barrier, 2 * REACH + ORB - 1)

    pending = []

    def push(src, dst, orb, dom):
        i = len(pending)
        copy = pltpu.make_async_remote_copy(
            src_ref=src,
            dst_ref=dst,
            send_sem=send.at[i],
            recv_sem=recv.at[i],
            device_id={"orb": orb, "dom": dom},
            device_id_type=pl.DeviceIdType.MESH,
        )
        copy.start()
        pending.append(copy)
        return copy

    def mate(k):
        return lax.rem(x + k, RING)

    upper = x >= RING // 2
    beyond = lax.rem(g + jnp.where(upper, 1, GROUPS - 1), GROUPS)
    beyond_at = jnp.where(upper, SLAB * (x - RING // 2), WIDE + GROUP + SLAB * x)
    group_at = WIDE + SLAB * x

    row, col = iota((2 * NZ, NZ), 0), iota((2 * NZ, NZ), 1)
    down_fine = jnp.where(row // 2 == col, 0.125, 0.0).astype(jnp.float32)
    row, col = iota((NZ, NZ), 0), iota((NZ, NZ), 1)
    down_mid = jnp.where((row % 64) // 2 == col, 0.125, 0.0).astype(jnp.float32)
    up_low = jnp.where(row == (col % 64) // 2, 1.0, 0.0).astype(jnp.float32)
    row, col = iota((NZ, 2 * NZ), 0), iota((NZ, 2 * NZ), 1)
    up_mid = jnp.where(row == col // 2, 1.0, 0.0).astype(jnp.float32)

    def fine_range(lo, hi, body):
        begin = jnp.maximum(lo, WIDE - SLAB * d)
        end = jnp.minimum(hi, WIDE + NX - SLAB * d)

        def run(p, carry):
            body(p)
            return carry

        lax.fori_loop(begin, end, run, 0)

    def sweep_fine(step, src, dst, lo, hi):
        def body(p):
            u, beside = beside_fine(src, p)
            dst[p] = KEEP * u + RELAX * (f[step, p] + beside)

        fine_range(lo, hi, body)

    def coarse_source(step, cycle, v):
        sides = []
        for pair in range(2):
            total = None
            for p in (WIDE + 2 * pair, WIDE + 2 * pair + 1):
                u, beside = beside_fine(v, p)
                r = f[step, p] - (6.0 * u - beside)
                total = r if total is None else total + r
            sides.append(total)
        tmp_res[...] = dot(jnp.concatenate(sides, axis=1), down_fine)
        c1[step, cycle, REACH] = tmp_res[pl.ds(0, Y1, 2)] + tmp_res[pl.ds(1, Y1, 2)]
        copies = []
        reach = REACH if cycle == 0 else REACH - 1
        for k in range(1, reach + 1):
            src = c1.at[step, cycle, REACH]
            copies.append(push(src, c1.at[step, cycle, REACH - k], o, lax.rem(d + k, DOM)))
            copies.append(push(src, c1.at[step, cycle, REACH + k], o, lax.rem(d + DOM - k, DOM)))
        return copies

    def coarse_solve(step, cycle, lo, hi):
        if cycle == 1:
            c1[step, cycle, 0] = jnp.zeros((Y1, NZ), jnp.float32)
            c1[step, cycle, SLABS - 1] = jnp.zeros((Y1, NZ), jnp.float32)
        mid = slice(1, SLABS + 1)

        def source():
            return c1[step, cycle]

        def sweep(src, dst):
            u, beside = beside_mid(src)
            dst[mid] = (KEEP * u + RELAX * (4.0 * source() + beside)) * mask1[...]

        m_a[mid] = (4.0 * RELAX) * source() * mask1[...]
        sweep(m_a, m_b)
        u, beside = beside_mid(m_b)
        r = source() - 0.25 * (6.0 * u - beside)
        tmp_mid[...] = dot(r.reshape(SLABS * Y1, NZ), down_mid)
        low = tmp_mid[pl.ds(0, SLABS * Y2, 2)] + tmp_mid[pl.ds(1, SLABS * Y2, 2)]
        tmp_low[...] = low.reshape(SLABS, Y2, NZ)
        l_a[mid] = (16.0 * RELAX) * tmp_low[...] * mask2[...]
        src, dst = l_a, l_b
        for unused in range(3):
            u, beside = beside_low(src)
            dst[mid] = (KEEP * u + RELAX * (16.0 * tmp_low[...] + beside)) * mask2[...]
            src, dst = dst, src
        wide = dot(src[mid].reshape(SLABS * Y2, NZ), up_low)
        tmp_mid[pl.ds(0, SLABS * Y2, 2)] = wide
        tmp_mid[pl.ds(1, SLABS * Y2, 2)] = wide
        m_a[mid] = m_b[mid] + tmp_mid[...].reshape(SLABS, Y1, NZ)
        sweep(m_a, m_b)
        sweep(m_b, m_a)
        count = hi - lo
        fine = dot(m_a[1 + lo : 1 + hi].reshape(count * Y1, NZ), up_mid)
        for j in range(count):
            for side in range(2):
                piece = fine[j * Y1 : (j + 1) * Y1, side * NZ : (side + 1) * NZ]
                up[2 * j + side, pl.ds(0, Y1, 2)] = piece
                up[2 * j + side, pl.ds(1, Y1, 2)] = piece

    def add_up(v, lo, hi, base):
        def body(p):
            v[p] = v[p] + up[(p - base) // 2]

        fine_range(lo, hi, body)

    def solve(step):
        swap = push(part.at[step], d1.at[step], o + 1 - 2 * lax.rem(o, 2), d)
        swap.wait_recv()
        for p in range(SLAB):
            half[step, p] = part[step, p] + d1[step, p]
        swap = push(half.at[step], d2.at[step], lax.rem(o + 2, ORB), d)
        swap.wait_recv()
        for p in range(SLAB):
            f[step, WIDE + p] = COUPLING * (half[step, p] + d2[step, p])

        after = [lax.rem(d + k, DOM) for k in (1, 2)]
        before = [lax.rem(d + DOM - k, DOM) for k in (1, 2)]
        fs = f.at[step]
        near = [
            push(fs.at[pl.ds(WIDE + 2, 2)], fs.at[pl.ds(WIDE - 2, 2)], o, after[0]),
            push(fs.at[pl.ds(WIDE, 2)], fs.at[pl.ds(WIDE + SLAB, 2)], o, before[0]),
        ]
        far = [
            push(fs.at[pl.ds(WIDE, 2)], fs.at[pl.ds(WIDE - 4, 2)], o, after[0]),
            push(fs.at[pl.ds(WIDE + 2, 2)], fs.at[pl.ds(WIDE + SLAB + 2, 2)], o, before[0]),
            push(fs.at[pl.ds(WIDE, 4)], fs.at[pl.ds(WIDE - 8, 4)], o, after[1]),
            push(fs.at[pl.ds(WIDE, 4)], fs.at[pl.ds(WIDE + SLAB + 4, 4)], o, before[1]),
        ]

        def first(lo, hi):
            def body(p):
                va[p] = RELAX * f[step, p]

            fine_range(lo, hi, body)

        for copy in near:
            copy.wait_recv()
        first(6, 14)
        sweep_fine(step, va, vb, 7, 13)
        copies = coarse_source(step, 0, vb)
        for copy in far:
            copy.wait_recv()
        first(1, 6)
        first(14, 19)
        sweep_fine(step, va, vb, 2, 7)
        sweep_fine(step, va, vb, 13, 18)
        for copy in copies:
            copy.wait_recv()
        coarse_solve(step, 0, REACH - 2, REACH + 3)
        add_up(vb, 2, 18, 0)
        sweep_fine(step, vb, va, 3, 17)
        sweep_fine(step, va, vb, 4, 16)
        sweep_fine(step, vb, va, 5, 15)
        sweep_fine(step, va, vb, 6, 14)
        copies = coarse_source(step, 1, vb)
        for copy in copies:
            copy.wait_recv()
        coarse_solve(step, 1, REACH - 1, REACH + 2)
        add_up(vb, 6, 14, 4)
        sweep_fine(step, vb, va, 7, 13)
        sweep_fine(step, va, vb, 8, 12)

    def spread_potential(step):
        for p in range(SLAB):
            place = (SLAB * d + p).astype(jnp.float32)
            dipole = (place + 0.5) * (2.0 / NX) - 1.0
            pot[step, group_at + p] = ext[p] + vb[WIDE + p] + control[step] * dipole
        src = pot.at[step, pl.ds(group_at, SLAB)]
        copies = []
        for k in range(RING):
            copies.append(
                push(src, pot.at[step, pl.ds(beyond_at, SLAB)], o, RING * beyond + mate(k))
            )
        for k in range(1, RING):
            copies.append(push(src, src, o, RING * g + mate(k)))
        return copies

    def image(src, c, p, full):
        u = src[c, p]
        near = src[c, p - 1] + src[c, p + 1] + plane_pair(u, 1)
        far = src[c, p - 2] + src[c, p + 2] + plane_pair(u, 2)
        return full * u - (2.0 / 3.0) * near + (1.0 / 24.0) * far

    def group_range(lo, hi, body):
        begin = jnp.maximum(lo, WIDE - GROUP * g)
        end = jnp.minimum(hi, WIDE + NX - GROUP * g)

        def run(p, carry):
            body(p)
            return carry

        lax.fori_loop(begin, end, run, 0)

    def propagate(step):
        now = psi.at[step]
        for order, (src, dst) in enumerate(((now, t1), (t1, t2), (t2, t3)), 1):
            factor = TIME_STEP / order

            def body(p):
                full = pot[step, p] + 3.75
                dst[0, p] = factor * image(src, 1, p, full)
                dst[1, p] = -factor * image(src, 0, p, full)

            group_range(2 * order, EXT - 2 * order, body)
        factor = TIME_STEP / TERMS

        def last(p):
            full = pot[step, p] + 3.75
            re = factor * image(t3, 1, p, full)
            im = -factor * image(t3, 0, p, full)
            psi[step + 1, 0, p] = psi[step, 0, p] + t1[0, p] + t2[0, p] + t3[0, p] + re
            psi[step + 1, 1, p] = psi[step, 1, p] + t1[1, p] + t2[1, p] + t3[1, p] + im

        group_range(2 * TERMS, EXT - 2 * TERMS, last)

    moves = []
    for k in range(RING):
        to = mate(k)
        moves.append(
            push(
                psi_in.at[:, to],
                psi.at[0, :, pl.ds(beyond_at, SLAB)],
                o,
                RING * beyond + to,
            )
        )
    for k in range(1, RING):
        to = mate(k)
        moves.append(
            push(psi_in.at[:, to], psi.at[0, :, pl.ds(group_at, SLAB)], o, RING * g + to)
        )

    for step in range(STEPS):
        solve(step)
        spread = spread_potential(step)
        for copy in moves:
            copy.wait_recv()
        if step == 0:
            own.wait()

        @pl.when(g == 0)
        def _():
            clear_halo(0, (psi.at[step],))

        @pl.when(g == GROUPS - 1)
        def _():
            clear_halo(WIDE + GROUP, (psi.at[step],))

        for copy in spread:
            copy.wait_recv()
        propagate(step)
        if step == STEPS - 1:
            break
        later = psi.at[step + 1]

        def density(p, carry):
            re, im = psi[step + 1, 0, WIDE + p], psi[step + 1, 1, WIDE + p]
            ringpart[p] = weight(x) * (re * re + im * im)
            return carry

        lax.fori_loop(0, GROUP, density, 0)
        shares = []
        for k in range(1, RING):
            to = mate(k)
            shares.append(
                push(ringpart.at[pl.ds(SLAB * to, SLAB)], ringpart.at[pl.ds(GROUP + SLAB * (k - 1), SLAB)], o, RING * g + to)
            )
        for copy in shares:
            copy.wait_recv()
        for p in range(SLAB):
            total = ringpart[SLAB * x + p]
            for k in range(1, RING):
                total = total + ringpart[GROUP + SLAB * (k - 1) + p]
            part[step + 1, p] = total
        moves = [
            push(
                later.at[:, pl.ds(GROUP, WIDE)],
                later.at[:, pl.ds(0, WIDE)],
                o,
                lax.rem(d + RING, DOM),
            ),
            push(
                later.at[:, pl.ds(WIDE, WIDE)],
                later.at[:, pl.ds(WIDE + GROUP, WIDE)],
                o,
                lax.rem(d + DOM - RING, DOM),
            ),
        ]

    hartree_out[...] = vb[WIDE : WIDE + SLAB]
    final = psi.at[STEPS]
    own = pltpu.make_async_copy(
        final.at[:, pl.ds(group_at, SLAB)], psi_out.at[:, x], local_sem.at[1]
    )
    own.start()
    moves = []
    for k in range(1, RING):
        to = mate(k)
        moves.append(
            push(
                final.at[:, pl.ds(WIDE + SLAB * to, SLAB)], psi_out.at[:, x], o, RING * g + to
            )
        )
    for copy in moves:
        copy.wait_recv()
    own.wait()
    for copy in pending:
        copy.wait_send()


def per_device(orbitals, occupations, external, control):
    f32 = jnp.float32
    vmem = pl.BlockSpec(memory_space=pltpu.VMEM)
    smem = pl.BlockSpec(memory_space=pltpu.SMEM)
    fields = pltpu.VMEM((2, EXT, NY, NZ), f32)
    slab = pltpu.VMEM((STEPS, SLAB, NY, NZ), f32)
    mid = pltpu.VMEM((SLABS + 2, Y1, NZ), f32)
    low = pltpu.VMEM((SLABS + 2, Y2, NZ), f32)
    return pl.pallas_call(
        kernel,
        out_shape=(
            jax.ShapeDtypeStruct(orbitals.shape, f32),
            jax.ShapeDtypeStruct(external.shape, f32),
        ),
        in_specs=[vmem, smem, vmem, smem],
        out_specs=(pl.BlockSpec(memory_space=pl.ANY), vmem),
        scratch_shapes=[
            pltpu.VMEM((STEPS + 1, 2, EXT, NY, NZ), f32),
            fields, fields, fields,
            pltpu.VMEM((STEPS, EXT, NY, NZ), f32),
            slab,
            pltpu.VMEM((GROUP + SLAB * (RING - 1), NY, NZ), f32),
            slab, slab, slab,
            pltpu.VMEM((STEPS, FEXT, NY, NZ), f32),
            pltpu.VMEM((FEXT, NY, NZ), f32),
            pltpu.VMEM((FEXT, NY, NZ), f32),
            pltpu.VMEM((STEPS, 2, SLABS, Y1, NZ), f32),
            mid, mid, low, low,
            pltpu.VMEM((SLABS, Y1, NZ), f32),
            pltpu.VMEM((SLABS, Y2, NZ), f32),
            pltpu.VMEM((NY, NZ), f32),
            pltpu.VMEM((SLABS * Y1, NZ), f32),
            pltpu.VMEM((SLABS, Y2, NZ), f32),
            pltpu.VMEM((10, NY, NZ), f32),
            pltpu.SemaphoreType.DMA((COPIES,)),
            pltpu.SemaphoreType.DMA((COPIES,)),
            pltpu.SemaphoreType.DMA((2,)),
        ],
        compiler_params=pltpu.CompilerParams(
            collective_id=0, has_side_effects=True, vmem_limit_bytes=56 * 1024 * 1024
        ),
    )(orbitals, occupations, external, control)


def solution(mesh):
    in_specs = (P(None, "orb", "dom", None, None), P("orb"), P("dom", None, None), P())
    out_specs = (P(None, "orb", "dom", None, None), P("dom", None, None))
    return jax.shard_map(
        per_device, mesh=mesh, in_specs=in_specs, out_specs=out_specs, check_vma=False
    )
```

```python
import functools

import jax
import jax.numpy as jnp
from jax import lax
from jax.experimental import pallas as pl
from jax.experimental.pallas import tpu as pltpu
from jax.sharding import PartitionSpec as P

STEPS = 2
TERMS = 4
TIME_STEP = 0.2
COUPLING = 0.025
RELAX = 0.8 / 6.0
KEEP = 0.2

ORB = 4
DOM = 64
RING = 4
GROUPS = DOM // RING
SLAB = 4
GROUP = RING * SLAB
WIDE = 8
NX = DOM * SLAB
NY, NZ = 64, 128
EXT = GROUP + 2 * WIDE
FEXT = SLAB + 2 * WIDE
REACH = 7
SLABS = 2 * REACH + 1
Y1, Y2 = NY // 2, NY // 4
COPIES = 160
HIGH = lax.Precision.HIGHEST


def dot(a, b):
    return jnp.dot(a, b, precision=HIGH, preferred_element_type=jnp.float32)


def iota(shape, dim):
    return lax.broadcasted_iota(jnp.int32, shape, dim)


def shifted(u, reach, axis, first, last):
    size = u.shape[axis]
    place = iota(u.shape, axis)
    low = jnp.where(place >= first + reach, pltpu.roll(u, reach, axis), 0.0)
    high = jnp.where(place <= last - reach, pltpu.roll(u, size - reach, axis), 0.0)
    return low + high


def plane_pair(u, reach):
    return shifted(u, reach, 0, 0, NY - 1) + shifted(u, reach, 1, 0, NZ - 1)


def beside_fine(ref, p):
    u = ref[p]
    return u, ref[p - 1] + ref[p + 1] + plane_pair(u, 1)


def beside_mid(ref):
    u = ref[1 : SLABS + 1]
    lane = iota(u.shape, 2)
    inner = lane % 64
    across = jnp.where(lane < 64, ref[2 : SLABS + 2], ref[0:SLABS])
    total = pltpu.roll(u + across, 64, 2)
    total = total + shifted(u, 1, 1, 0, Y1 - 1)
    total = total + jnp.where(inner >= 1, pltpu.roll(u, 1, 2), 0.0)
    total = total + jnp.where(inner <= 62, pltpu.roll(u, 127, 2), 0.0)
    return u, total


def beside_low(ref):
    u = ref[1 : SLABS + 1]
    total = ref[2 : SLABS + 2] + ref[0:SLABS]
    total = total + shifted(u, 1, 1, 0, Y2 - 1) + shifted(u, 1, 2, 0, 31)
    return u, total


def kernel(
    psi_in, occ, ext, control, psi_out, hartree_out,
    psi, t1, t2, t3, pot, part, ringpart, half, d1, d2, f, va, vb, c1, m_a, m_b, l_a, l_b, mask1, mask2,
    tmp_res, tmp_mid, tmp_low, up, send, recv, local_sem,
):
    o = lax.axis_index("orb")
    d = lax.axis_index("dom")
    x = lax.rem(d, RING)
    g = lax.div(d, RING)

    barrier = pltpu.get_barrier_semaphore()
    for k in range(1, REACH + 1):
        for to in (lax.rem(d + k, DOM), lax.rem(d + DOM - k, DOM)):
            pl.semaphore_signal(barrier, inc=1, device_id={"orb": o, "dom": to})
    for k in range(1, ORB):
        pl.semaphore_signal(barrier, inc=1, device_id={"orb": lax.rem(o + k, ORB), "dom": d})

    own = pltpu.make_async_copy(
        psi_in.at[:, x], psi.at[0, :, pl.ds(WIDE + SLAB * x, SLAB)], local_sem.at[0]
    )
    own.start()

    def weight(b):
        return occ[b].astype(jnp.float32) * (1.0 / 16.0)

    for p in range(SLAB):
        total = jnp.zeros((NY, NZ), jnp.float32)
        for b in range(4):
            re, im = psi_in[0, b, p], psi_in[1, b, p]
            total = total + weight(b) * (re * re + im * im)
        part[0, p] = total

    for s in range(SLABS):
        inside = jnp.logical_and(d - REACH + s >= 0, d - REACH + s < DOM)
        factor = jnp.where(inside, 1.0, 0.0).astype(jnp.float32)
        mask1[s] = jnp.full((Y1, NZ), 1.0, jnp.float32) * factor
        mask2[s] = jnp.full((Y2, NZ), 1.0, jnp.float32) * factor
    for ref in (m_a, m_b, l_a, l_b):
        ref[0] = jnp.zeros(ref.shape[1:], jnp.float32)
        ref[SLABS + 1] = jnp.zeros(ref.shape[1:], jnp.float32)

    def clear_fine(p, carry):
        va[p] = jnp.zeros((NY, NZ), jnp.float32)
        vb[p] = jnp.zeros((NY, NZ), jnp.float32)
        return carry

    lax.fori_loop(0, FEXT, clear_fine, 0)

    def clear_halo(begin, refs):
        def body(p, carry):
            for ref in refs:
                for c in range(2):
                    ref[c, p] = jnp.zeros((NY, NZ), jnp.float32)
            return carry

        lax.fori_loop(begin, begin + WIDE, body, 0)

    @pl.when(g == 0)
    def _():
        clear_halo(0, (t1, t2, t3))

    @pl.when(g == GROUPS - 1)
    def _():
        clear_halo(WIDE + GROUP, (t1, t2, t3))

    pl.semaphore_wait(barrier, 2 * REACH + ORB - 1)

    pending = []

    def push(src, dst, orb, dom):
        i = len(pending)
        copy = pltpu.make_async_remote_copy(
            src_ref=src,
            dst_ref=dst,
            send_sem=send.at[i],
            recv_sem=recv.at[i],
            device_id={"orb": orb, "dom": dom},
            device_id_type=pl.DeviceIdType.MESH,
        )
        copy.start()
        pending.append(copy)
        return copy

    def mate(k):
        return lax.rem(x + k, RING)

    after_group, before_group = lax.rem(d + RING, DOM), lax.rem(d + DOM - RING, DOM)
    group_at = WIDE + SLAB * x

    row, col = iota((2 * NZ, NZ), 0), iota((2 * NZ, NZ), 1)
    down_fine = jnp.where(row // 2 == col, 0.125, 0.0).astype(jnp.float32)
    row, col = iota((NZ, NZ), 0), iota((NZ, NZ), 1)
    down_mid = jnp.where((row % 64) // 2 == col, 0.125, 0.0).astype(jnp.float32)
    up_low = jnp.where(row == (col % 64) // 2, 1.0, 0.0).astype(jnp.float32)
    row, col = iota((NZ, 2 * NZ), 0), iota((NZ, 2 * NZ), 1)
    up_mid = jnp.where(row == col // 2, 1.0, 0.0).astype(jnp.float32)

    def fine_range(lo, hi, body):
        begin = jnp.maximum(lo, WIDE - SLAB * d)
        end = jnp.minimum(hi, WIDE + NX - SLAB * d)

        def run(p, carry):
            body(p)
            return carry

        lax.fori_loop(begin, end, run, 0)

    def sweep_fine(step, src, dst, lo, hi):
        def body(p):
            u, beside = beside_fine(src, p)
            dst[p] = KEEP * u + RELAX * (f[step, p] + beside)

        fine_range(lo, hi, body)

    def coarse_source(step, cycle, v):
        sides = []
        for pair in range(2):
            total = None
            for p in (WIDE + 2 * pair, WIDE + 2 * pair + 1):
                u, beside = beside_fine(v, p)
                r = f[step, p] - (6.0 * u - beside)
                total = r if total is None else total + r
            sides.append(total)
        tmp_res[...] = dot(jnp.concatenate(sides, axis=1), down_fine)
        c1[step, cycle, REACH] = tmp_res[pl.ds(0, Y1, 2)] + tmp_res[pl.ds(1, Y1, 2)]
        copies = []
        reach = REACH if cycle == 0 else REACH - 1
        for k in range(1, reach + 1):
            src = c1.at[step, cycle, REACH]
            copies.append(push(src, c1.at[step, cycle, REACH - k], o, lax.rem(d + k, DOM)))
            copies.append(push(src, c1.at[step, cycle, REACH + k], o, lax.rem(d + DOM - k, DOM)))
        return copies

    def coarse_solve(step, cycle, lo, hi):
        if cycle == 1:
            c1[step, cycle, 0] = jnp.zeros((Y1, NZ), jnp.float32)
            c1[step, cycle, SLABS - 1] = jnp.zeros((Y1, NZ), jnp.float32)
        mid = slice(1, SLABS + 1)

        def source():
            return c1[step, cycle]

        def sweep(src, dst):
            u, beside = beside_mid(src)
            dst[mid] = (KEEP * u + RELAX * (4.0 * source() + beside)) * mask1[...]

        m_a[mid] = (4.0 * RELAX) * source() * mask1[...]
        sweep(m_a, m_b)
        u, beside = beside_mid(m_b)
        r = source() - 0.25 * (6.0 * u - beside)
        tmp_mid[...] = dot(r.reshape(SLABS * Y1, NZ), down_mid)
        low = tmp_mid[pl.ds(0, SLABS * Y2, 2)] + tmp_mid[pl.ds(1, SLABS * Y2, 2)]
        tmp_low[...] = low.reshape(SLABS, Y2, NZ)
        l_a[mid] = (16.0 * RELAX) * tmp_low[...] * mask2[...]
        src, dst = l_a, l_b
        for unused in range(3):
            u, beside = beside_low(src)
            dst[mid] = (KEEP * u + RELAX * (16.0 * tmp_low[...] + beside)) * mask2[...]
            src, dst = dst, src
        wide = dot(src[mid].reshape(SLABS * Y2, NZ), up_low)
        tmp_mid[pl.ds(0, SLABS * Y2, 2)] = wide
        tmp_mid[pl.ds(1, SLABS * Y2, 2)] = wide
        m_a[mid] = m_b[mid] + tmp_mid[...].reshape(SLABS, Y1, NZ)
        sweep(m_a, m_b)
        sweep(m_b, m_a)
        count = hi - lo
        fine = dot(m_a[1 + lo : 1 + hi].reshape(count * Y1, NZ), up_mid)
        for j in range(count):
            for side in range(2):
                piece = fine[j * Y1 : (j + 1) * Y1, side * NZ : (side + 1) * NZ]
                up[2 * j + side, pl.ds(0, Y1, 2)] = piece
                up[2 * j + side, pl.ds(1, Y1, 2)] = piece

    def add_up(v, lo, hi, base):
        def body(p):
            v[p] = v[p] + up[(p - base) // 2]

        fine_range(lo, hi, body)

    def solve(step, meanwhile):
        swap = push(part.at[step], d1.at[step], o + 1 - 2 * lax.rem(o, 2), d)
        swap.wait_recv()
        for p in range(SLAB):
            half[step, p] = part[step, p] + d1[step, p]
        swap = push(half.at[step], d2.at[step], lax.rem(o + 2, ORB), d)
        swap.wait_recv()
        for p in range(SLAB):
            f[step, WIDE + p] = COUPLING * (half[step, p] + d2[step, p])

        after = [lax.rem(d + k, DOM) for k in (1, 2)]
        before = [lax.rem(d + DOM - k, DOM) for k in (1, 2)]
        fs = f.at[step]
        near = [
            push(fs.at[pl.ds(WIDE + 2, 2)], fs.at[pl.ds(WIDE - 2, 2)], o, after[0]),
            push(fs.at[pl.ds(WIDE, 2)], fs.at[pl.ds(WIDE + SLAB, 2)], o, before[0]),
        ]
        far = [
            push(fs.at[pl.ds(WIDE, 2)], fs.at[pl.ds(WIDE - 4, 2)], o, after[0]),
            push(fs.at[pl.ds(WIDE + 2, 2)], fs.at[pl.ds(WIDE + SLAB + 2, 2)], o, before[0]),
            push(fs.at[pl.ds(WIDE, 4)], fs.at[pl.ds(WIDE - 8, 4)], o, after[1]),
            push(fs.at[pl.ds(WIDE, 4)], fs.at[pl.ds(WIDE + SLAB + 4, 4)], o, before[1]),
        ]

        def first(lo, hi):
            def body(p):
                va[p] = RELAX * f[step, p]

            fine_range(lo, hi, body)

        for copy in near:
            copy.wait_recv()
        first(6, 14)
        sweep_fine(step, va, vb, 7, 13)
        copies = coarse_source(step, 0, vb)
        meanwhile()
        for copy in far:
            copy.wait_recv()
        first(1, 6)
        first(14, 19)
        sweep_fine(step, va, vb, 2, 7)
        sweep_fine(step, va, vb, 13, 18)
        for copy in copies:
            copy.wait_recv()
        coarse_solve(step, 0, REACH - 2, REACH + 3)
        add_up(vb, 2, 18, 0)
        sweep_fine(step, vb, va, 3, 17)
        sweep_fine(step, va, vb, 4, 16)
        sweep_fine(step, vb, va, 5, 15)
        sweep_fine(step, va, vb, 6, 14)
        copies = coarse_source(step, 1, vb)
        for copy in copies:
            copy.wait_recv()
        coarse_solve(step, 1, REACH - 1, REACH + 2)
        add_up(vb, 6, 14, 4)
        sweep_fine(step, vb, va, 7, 13)
        sweep_fine(step, va, vb, 8, 12)

    def spread_potential(step):
        for p in range(SLAB):
            place = (SLAB * d + p).astype(jnp.float32)
            dipole = (place + 0.5) * (2.0 / NX) - 1.0
            pot[step, group_at + p] = ext[p] + vb[WIDE + p] + control[step] * dipole
        src = pot.at[step, pl.ds(group_at, SLAB)]
        return [push(src, src, o, RING * g + mate(k)) for k in range(1, RING)]

    def spread_halo(step):
        at = pot.at[step]
        return [
            push(at.at[pl.ds(WIDE + GROUP - 6, 6)], at.at[pl.ds(WIDE - 6, 6)], o, after_group),
            push(at.at[pl.ds(WIDE, 6)], at.at[pl.ds(WIDE + GROUP, 6)], o, before_group),
        ]

    def low_halo(ref):
        return push(ref.at[:, pl.ds(GROUP, WIDE)], ref.at[:, pl.ds(0, WIDE)], o, after_group)

    def high_halo(ref):
        return push(
            ref.at[:, pl.ds(WIDE, WIDE)], ref.at[:, pl.ds(WIDE + GROUP, WIDE)], o, before_group
        )

    def image(src, c, p, full):
        u = src[c, p]
        near = src[c, p - 1] + src[c, p + 1] + plane_pair(u, 1)
        far = src[c, p - 2] + src[c, p + 2] + plane_pair(u, 2)
        return full * u - (2.0 / 3.0) * near + (1.0 / 24.0) * far

    def group_range(lo, hi, body):
        begin = jnp.maximum(lo, WIDE - GROUP * g)
        end = jnp.minimum(hi, WIDE + NX - GROUP * g)

        def run(p, carry):
            body(p)
            return carry

        lax.fori_loop(begin, end, run, 0)

    def term(step, order, lo, hi):
        src, dst = ((psi.at[step], t1), (t1, t2), (t2, t3), (t3, None))[order - 1]
        factor = TIME_STEP / order

        def body(p):
            full = pot[step, p] + 3.75
            re = factor * image(src, 1, p, full)
            im = -factor * image(src, 0, p, full)
            if order < TERMS:
                dst[0, p] = re
                dst[1, p] = im
                return
            re = re + (psi[step, 0, p] + t1[0, p]) + (t2[0, p] + t3[0, p])
            im = im + (psi[step, 1, p] + t1[1, p]) + (t2[1, p] + t3[1, p])
            psi[step + 1, 0, p] = re
            psi[step + 1, 1, p] = im
            if step < STEPS - 1:
                ringpart[p - WIDE] = weight(x) * (re * re + im * im)

        group_range(lo, hi, body)

    def inside(step):
        for order in range(1, TERMS + 1):
            cut = 2 * (order - 1)
            term(step, order, WIDE + cut, WIDE + GROUP - cut)

    def low_edge(step):
        for order in range(1, TERMS + 1):
            term(step, order, 2 * order, 2 * order + 6)

    def high_edge(step):
        for order in range(1, TERMS + 1):
            term(step, order, EXT - 6 - 2 * order, EXT - 2 * order)

    class Shares:
        def __init__(self, src_of, dst_of):
            self.copies = []
            for k in range(1, RING):
                to = mate(k)
                i = len(pending)
                copy = pltpu.make_async_remote_copy(
                    src_ref=src_of(to),
                    dst_ref=dst_of(k),
                    send_sem=send.at[i],
                    recv_sem=recv.at[i],
                    device_id={"orb": o, "dom": RING * g + to},
                    device_id_type=pl.DeviceIdType.MESH,
                )
                pending.append(copy)
                self.copies.append((to, copy))

        def begin(self, lo, hi):
            for to, copy in self.copies:
                pl.when(jnp.logical_and(to >= lo, to < hi))(copy.start)

        def wait(self):
            for unused, copy in self.copies:
                copy.wait_recv()

    regroup = []
    for k in range(1, RING):
        to = mate(k)
        regroup.append(
            push(psi_in.at[:, to], psi.at[0, :, pl.ds(group_at, SLAB)], o, RING * g + to)
        )
    halos = []

    def regrouped():
        for copy in regroup:
            copy.wait_recv()
        own.wait()
        halos.append(low_halo(psi.at[0]))
        halos.append(high_halo(psi.at[0]))

    for step in range(STEPS):
        solve(step, regrouped if step == 0 else lambda: None)
        for copy in spread_potential(step):
            copy.wait_recv()
        spread = spread_halo(step)
        for copy in halos:
            copy.wait_recv()

        @pl.when(g == 0)
        def _():
            clear_halo(0, (psi.at[step],))

        @pl.when(g == GROUPS - 1)
        def _():
            clear_halo(WIDE + GROUP, (psi.at[step],))

        inside(step)
        for copy in spread:
            copy.wait_recv()
        later = psi.at[step + 1]
        if step < STEPS - 1:
            shares = Shares(
                lambda to: ringpart.at[pl.ds(SLAB * to, SLAB)],
                lambda k: ringpart.at[pl.ds(GROUP + SLAB * (k - 1), SLAB)],
            )
        else:
            shares = Shares(
                lambda to: later.at[:, pl.ds(WIDE + SLAB * to, SLAB)],
                lambda k: psi_out.at[:, x],
            )
        low_edge(step)
        shares.begin(0, RING // 2)
        if step < STEPS - 1:
            halos = [high_halo(later)]
        high_edge(step)
        shares.begin(RING // 2, RING)
        if step < STEPS - 1:
            halos.append(low_halo(later))
            shares.wait()
            for p in range(SLAB):
                total = ringpart[SLAB * x + p]
                for k in range(1, RING):
                    total = total + ringpart[GROUP + SLAB * (k - 1) + p]
                part[step + 1, p] = total

    hartree_out[...] = vb[WIDE : WIDE + SLAB]
    final = psi.at[STEPS]
    own = pltpu.make_async_copy(
        final.at[:, pl.ds(group_at, SLAB)], psi_out.at[:, x], local_sem.at[1]
    )
    own.start()
    shares.wait()
    own.wait()
    for copy in pending:
        copy.wait_send()


def per_device(orbitals, occupations, external, control):
    f32 = jnp.float32
    vmem = pl.BlockSpec(memory_space=pltpu.VMEM)
    smem = pl.BlockSpec(memory_space=pltpu.SMEM)
    fields = pltpu.VMEM((2, EXT, NY, NZ), f32)
    slab = pltpu.VMEM((STEPS, SLAB, NY, NZ), f32)
    mid = pltpu.VMEM((SLABS + 2, Y1, NZ), f32)
    low = pltpu.VMEM((SLABS + 2, Y2, NZ), f32)
    return pl.pallas_call(
        kernel,
        out_shape=(
            jax.ShapeDtypeStruct(orbitals.shape, f32),
            jax.ShapeDtypeStruct(external.shape, f32),
        ),
        in_specs=[vmem, smem, vmem, smem],
        out_specs=(pl.BlockSpec(memory_space=pl.ANY), vmem),
        scratch_shapes=[
            pltpu.VMEM((STEPS + 1, 2, EXT, NY, NZ), f32),
            fields, fields, fields,
            pltpu.VMEM((STEPS, EXT, NY, NZ), f32),
            slab,
            pltpu.VMEM((GROUP + SLAB * (RING - 1), NY, NZ), f32),
            slab, slab, slab,
            pltpu.VMEM((STEPS, FEXT, NY, NZ), f32),
            pltpu.VMEM((FEXT, NY, NZ), f32),
            pltpu.VMEM((FEXT, NY, NZ), f32),
            pltpu.VMEM((STEPS, 2, SLABS, Y1, NZ), f32),
            mid, mid, low, low,
            pltpu.VMEM((SLABS, Y1, NZ), f32),
            pltpu.VMEM((SLABS, Y2, NZ), f32),
            pltpu.VMEM((NY, NZ), f32),
            pltpu.VMEM((SLABS * Y1, NZ), f32),
            pltpu.VMEM((SLABS, Y2, NZ), f32),
            pltpu.VMEM((10, NY, NZ), f32),
            pltpu.SemaphoreType.DMA((COPIES,)),
            pltpu.SemaphoreType.DMA((COPIES,)),
            pltpu.SemaphoreType.DMA((2,)),
        ],
        compiler_params=pltpu.CompilerParams(
            collective_id=0, has_side_effects=True, vmem_limit_bytes=56 * 1024 * 1024
        ),
    )(orbitals, occupations, external, control)


def solution(mesh):
    in_specs = (P(None, "orb", "dom", None, None), P("orb"), P("dom", None, None), P())
    out_specs = (P(None, "orb", "dom", None, None), P("dom", None, None))
    return jax.shard_map(
        per_device, mesh=mesh, in_specs=in_specs, out_specs=out_specs, check_vma=False
    )
```

```python
import functools

import jax
import jax.numpy as jnp
from jax import lax
from jax.experimental import pallas as pl
from jax.experimental.pallas import tpu as pltpu
from jax.sharding import PartitionSpec as P

STEPS = 2
TERMS = 4
TIME_STEP = 0.2
COUPLING = 0.025
RELAX = 0.8 / 6.0
KEEP = 0.2

ORB = 4
DOM = 64
RING = 4
GROUPS = DOM // RING
SLAB = 4
GROUP = RING * SLAB
WIDE = 8
NX = DOM * SLAB
NY, NZ = 64, 128
EXT = GROUP + 2 * WIDE
FEXT = SLAB + 2 * WIDE
REACH = 7
SLABS = 2 * REACH + 1
Y1, Y2 = NY // 2, NY // 4
COPIES = 160
HIGH = lax.Precision.HIGHEST


def dot(a, b):
    return jnp.dot(a, b, precision=HIGH, preferred_element_type=jnp.float32)


def iota(shape, dim):
    return lax.broadcasted_iota(jnp.int32, shape, dim)


def flipped(a, up):
    axis = a.ndim - 2
    place = iota(a.shape, axis)
    if up:
        return jnp.where(place <= 6, pltpu.roll(a, 7, axis), 0.0)
    return jnp.where(place >= 1, pltpu.roll(a, 1, axis), 0.0)


def rows(u, begin, count):
    return u[..., 8 * begin : 8 * (begin + count), :]


def y_pairs(u, reaches):
    tiles = u.shape[-2] // 8
    axis = u.ndim - 2
    first = [flipped(rows(u, i, 1), True) for i in range(reaches)]
    last = [flipped(rows(u, tiles - 1 - i, 1), False) for i in range(reaches)]
    sums = []
    for reach in range(1, reaches + 1):
        up = jnp.concatenate([rows(u, reach, tiles - reach)] + first[:reach], axis=axis)
        down = jnp.concatenate(last[:reach][::-1] + [rows(u, 0, tiles - reach)], axis=axis)
        sums.append(up + down)
    return sums


def z_pair(u, reach, period=NZ):
    axis = u.ndim - 1
    place = iota(u.shape, axis)
    if period < NZ:
        place = place % 64
    low = jnp.where(place >= reach, pltpu.roll(u, reach, axis), 0.0)
    high = jnp.where(place <= period - 1 - reach, pltpu.roll(u, NZ - reach, axis), 0.0)
    return low + high


def beside_fine(ref, p):
    u = ref[p]
    return u, (ref[p - 1] + ref[p + 1]) + (y_pairs(u, 1)[0] + z_pair(u, 1))


def beside_mid(ref):
    u = ref[1 : SLABS + 1]
    lane = iota(u.shape, 2)
    across = jnp.where(lane < 64, ref[2 : SLABS + 2], ref[0:SLABS])
    total = pltpu.roll(u + across, 64, 2)
    return u, total + (y_pairs(u, 1)[0] + z_pair(u, 1, 64))


def beside_low(ref):
    u = ref[1 : SLABS + 1]
    total = ref[2 : SLABS + 2] + ref[0:SLABS]
    return u, total + (y_pairs(u, 1)[0] + z_pair(u, 1, 32))


def halved(t):
    tiles = t.shape[-2] // 8
    pairs = [rows(t, 2 * i, 1) + rows(t, 2 * i + 1, 1) for i in range(tiles // 2)]
    return jnp.concatenate(pairs, axis=t.ndim - 2)


def doubled(t):
    tiles = t.shape[-2] // 8
    return jnp.concatenate([rows(t, i // 2, 1) for i in range(2 * tiles)], axis=t.ndim - 2)


def gathered(ref, *at):
    return jnp.concatenate([ref[(*at, pl.ds(v, 8, stride=8))] for v in range(8)], axis=0)


def scatter(ref, value, *at):
    for v in range(8):
        ref[(*at, pl.ds(v, 8, stride=8))] = value[8 * v : 8 * v + 8]


def kernel(
    psi_in, occ, ext, control, psi_out, hartree_out,
    psi, t1, t2, t3, pot, part, ringpart, half, d1, d2, f, va, vb, c1, m_a, m_b, l_a, l_b, mask1, mask2,
    land, plane, tmp_low, up, send, recv, local_sem,
):
    o = lax.axis_index("orb")
    d = lax.axis_index("dom")
    x = lax.rem(d, RING)
    g = lax.div(d, RING)

    barrier = pltpu.get_barrier_semaphore()
    for k in range(1, REACH + 1):
        for to in (lax.rem(d + k, DOM), lax.rem(d + DOM - k, DOM)):
            pl.semaphore_signal(barrier, inc=1, device_id={"orb": o, "dom": to})
    for k in range(1, ORB):
        pl.semaphore_signal(barrier, inc=1, device_id={"orb": lax.rem(o + k, ORB), "dom": d})

    own = pltpu.make_async_copy(
        psi_in.at[:, x], land.at[:, pl.ds(SLAB * x, SLAB)], local_sem.at[0]
    )
    own.start()

    def weight(b):
        return occ[b].astype(jnp.float32) * (1.0 / 16.0)

    for p in range(SLAB):
        total = jnp.zeros((NY, NZ), jnp.float32)
        for b in range(4):
            re, im = psi_in[0, b, p], psi_in[1, b, p]
            total = total + weight(b) * (re * re + im * im)
        plane[p] = total
        part[0, p] = gathered(plane, p)

    for s in range(SLABS):
        inside = jnp.logical_and(d - REACH + s >= 0, d - REACH + s < DOM)
        factor = jnp.where(inside, 1.0, 0.0).astype(jnp.float32)
        mask1[s] = jnp.full((Y1, NZ), 1.0, jnp.float32) * factor
        mask2[s] = jnp.full((Y2, NZ), 1.0, jnp.float32) * factor
    for ref in (m_a, m_b, l_a, l_b):
        ref[0] = jnp.zeros(ref.shape[1:], jnp.float32)
        ref[SLABS + 1] = jnp.zeros(ref.shape[1:], jnp.float32)

    def clear_fine(p, carry):
        va[p] = jnp.zeros((NY, NZ), jnp.float32)
        vb[p] = jnp.zeros((NY, NZ), jnp.float32)
        return carry

    lax.fori_loop(0, FEXT, clear_fine, 0)

    def clear_halo(begin, count, refs):
        def body(p, carry):
            for ref in refs:
                for c in range(2):
                    ref[c, p] = jnp.zeros((NY, NZ), jnp.float32)
            return carry

        lax.fori_loop(begin, begin + count, body, 0)

    @pl.when(g == 0)
    def _():
        clear_halo(0, WIDE, (t1, t2, t3))

    @pl.when(g == GROUPS - 1)
    def _():
        clear_halo(WIDE + GROUP, WIDE, (t1, t2, t3))

    pl.semaphore_wait(barrier, 2 * REACH + ORB - 1)

    pending = []

    def push(src, dst, orb, dom):
        i = len(pending)
        copy = pltpu.make_async_remote_copy(
            src_ref=src,
            dst_ref=dst,
            send_sem=send.at[i],
            recv_sem=recv.at[i],
            device_id={"orb": orb, "dom": dom},
            device_id_type=pl.DeviceIdType.MESH,
        )
        copy.start()
        pending.append(copy)
        return copy

    def mate(k):
        return lax.rem(x + k, RING)

    after_group, before_group = lax.rem(d + RING, DOM), lax.rem(d + DOM - RING, DOM)
    group_at = WIDE + SLAB * x
    core = lax.rem(o, 2)
    sibling = o + 1 - 2 * core

    row, col = iota((2 * NZ, NZ), 0), iota((2 * NZ, NZ), 1)
    down_fine = jnp.where(row // 2 == col, 0.125, 0.0).astype(jnp.float32)
    row, col = iota((NZ, NZ), 0), iota((NZ, NZ), 1)
    down_mid = jnp.where((row % 64) // 2 == col, 0.125, 0.0).astype(jnp.float32)
    up_low = jnp.where(row == (col % 64) // 2, 1.0, 0.0).astype(jnp.float32)
    row, col = iota((NZ, 2 * NZ), 0), iota((NZ, 2 * NZ), 1)
    up_mid = jnp.where(row == col // 2, 1.0, 0.0).astype(jnp.float32)

    def fine_range(lo, hi, body):
        begin = jnp.maximum(lo, WIDE - SLAB * d)
        end = jnp.minimum(hi, WIDE + NX - SLAB * d)

        def run(p, carry):
            body(p)
            return carry

        lax.fori_loop(begin, end, run, 0)

    def sweep_fine(step, src, dst, lo, hi):
        def body(p):
            u, beside = beside_fine(src, p)
            dst[p] = KEEP * u + RELAX * (f[step, p] + beside)

        fine_range(lo, hi, body)

    def coarse_source(step, cycle, v):
        sides = []
        for pair in range(2):
            total = None
            for p in (WIDE + 2 * pair, WIDE + 2 * pair + 1):
                u, beside = beside_fine(v, p)
                r = f[step, p] - (6.0 * u - beside)
                total = r if total is None else total + r
            sides.append(halved(total))
        c1[step, cycle, REACH] = dot(jnp.concatenate(sides, axis=1), down_fine).reshape(2, Y2, NZ)
        copies = []
        reach = REACH if cycle == 0 else REACH - 1
        for k in range(1, reach + 1):
            src = c1.at[step, cycle, REACH, core]
            low = c1.at[step, cycle, REACH - k, core]
            high = c1.at[step, cycle, REACH + k, core]
            copies.append(push(src, low, o, lax.rem(d + k, DOM)))
            copies.append(push(src, high, o, lax.rem(d + DOM - k, DOM)))
        return copies

    def whole_source(step, cycle, copies):
        for copy in copies:
            copy.wait_recv()
        reach = len(copies) // 2
        swaps = []
        for begin in (REACH - reach, REACH + 1):
            piece = c1.at[step, cycle, pl.ds(begin, reach), core]
            swaps.append(push(piece, piece, sibling, d))
        for copy in swaps:
            copy.wait_recv()

    def coarse_solve(step, cycle, lo, hi):
        if cycle == 1:
            c1[step, cycle, 0] = jnp.zeros((2, Y2, NZ), jnp.float32)
            c1[step, cycle, SLABS - 1] = jnp.zeros((2, Y2, NZ), jnp.float32)
        mid = slice(1, SLABS + 1)

        def source():
            return c1[step, cycle].reshape(SLABS, Y1, NZ)

        def sweep(src, dst):
            u, beside = beside_mid(src)
            dst[mid] = (KEEP * u + RELAX * (4.0 * source() + beside)) * mask1[...]

        m_a[mid] = (4.0 * RELAX) * source() * mask1[...]
        sweep(m_a, m_b)
        u, beside = beside_mid(m_b)
        r = source() - 0.25 * (6.0 * u - beside)
        low = dot(halved(r).reshape(SLABS * Y2, NZ), down_mid)
        tmp_low[...] = low.reshape(SLABS, Y2, NZ)
        l_a[mid] = (16.0 * RELAX) * tmp_low[...] * mask2[...]
        src, dst = l_a, l_b
        for unused in range(3):
            u, beside = beside_low(src)
            dst[mid] = (KEEP * u + RELAX * (16.0 * tmp_low[...] + beside)) * mask2[...]
            src, dst = dst, src
        wide = dot(src[mid].reshape(SLABS * Y2, NZ), up_low)
        m_a[mid] = m_b[mid] + doubled(wide.reshape(SLABS, Y2, NZ))
        sweep(m_a, m_b)
        sweep(m_b, m_a)
        count = hi - lo
        fine = dot(m_a[1 + lo : 1 + hi].reshape(count * Y1, NZ), up_mid)
        for j in range(count):
            for side in range(2):
                piece = fine[j * Y1 : (j + 1) * Y1, side * NZ : (side + 1) * NZ]
                up[2 * j + side] = doubled(piece)

    def add_up(v, lo, hi, base):
        def body(p):
            v[p] = v[p] + up[(p - base) // 2]

        fine_range(lo, hi, body)

    def solve(step, meanwhile):
        swap = push(part.at[step], d1.at[step], sibling, d)
        swap.wait_recv()
        for p in range(SLAB):
            half[step, p] = part[step, p] + d1[step, p]
        swap = push(half.at[step], d2.at[step], lax.rem(o + 2, ORB), d)
        swap.wait_recv()
        for p in range(SLAB):
            f[step, WIDE + p] = COUPLING * (half[step, p] + d2[step, p])

        meanwhile('density')
        after = [lax.rem(d + k, DOM) for k in (1, 2)]
        before = [lax.rem(d + DOM - k, DOM) for k in (1, 2)]
        fs = f.at[step]
        near = [
            push(fs.at[pl.ds(WIDE + 2, 2)], fs.at[pl.ds(WIDE - 2, 2)], o, after[0]),
            push(fs.at[pl.ds(WIDE, 2)], fs.at[pl.ds(WIDE + SLAB, 2)], o, before[0]),
        ]
        far = [
            push(fs.at[pl.ds(WIDE + core, 1)], fs.at[pl.ds(WIDE - 4 + core, 1)], o, after[0]),
            push(fs.at[pl.ds(WIDE + 2 + core, 1)], fs.at[pl.ds(14 + core, 1)], o, before[0]),
            push(fs.at[pl.ds(WIDE + 2 * core, 2)], fs.at[pl.ds(2 * core, 2)], o, after[1]),
            push(fs.at[pl.ds(WIDE + 2 * core, 2)], fs.at[pl.ds(16 + 2 * core, 2)], o, before[1]),
        ]

        meanwhile('near')

        def first(lo, hi):
            def body(p):
                va[p] = RELAX * f[step, p]

            fine_range(lo, hi, body)

        for copy in near:
            copy.wait_recv()
        first(6, 14)
        sweep_fine(step, va, vb, 7, 13)
        copies = coarse_source(step, 0, vb)
        meanwhile('source')
        for copy in far:
            copy.wait_recv()
        far = []
        for at, count in ((4 + core, 1), (14 + core, 1), (2 * core, 2), (16 + 2 * core, 2)):
            piece = fs.at[pl.ds(at, count)]
            far.append(push(piece, piece, sibling, d))
        for copy in far:
            copy.wait_recv()
        first(1, 6)
        first(14, 19)
        sweep_fine(step, va, vb, 2, 7)
        sweep_fine(step, va, vb, 13, 18)
        whole_source(step, 0, copies)
        coarse_solve(step, 0, REACH - 2, REACH + 3)
        add_up(vb, 2, 18, 0)
        sweep_fine(step, vb, va, 3, 17)
        sweep_fine(step, va, vb, 4, 16)
        sweep_fine(step, vb, va, 5, 15)
        sweep_fine(step, va, vb, 6, 14)
        copies = coarse_source(step, 1, vb)
        meanwhile('again')
        whole_source(step, 1, copies)
        meanwhile('whole')
        coarse_solve(step, 1, REACH - 1, REACH + 2)
        add_up(vb, 6, 14, 4)
        sweep_fine(step, vb, va, 7, 13)
        sweep_fine(step, va, vb, 8, 12)

    def spread_potential(step):
        for p in range(SLAB):
            place = (SLAB * d + p).astype(jnp.float32)
            dipole = (place + 0.5) * (2.0 / NX) - 1.0
            pot[step, group_at + p] = gathered(ext, p) + vb[WIDE + p] + control[step] * dipole
        src = pot.at[step, pl.ds(group_at, SLAB)]
        return [push(src, src, o, RING * g + mate(k)) for k in range(1, RING)]

    def spread_halo(step):
        at = pot.at[step]
        return [
            push(at.at[pl.ds(WIDE + GROUP - 6, 6)], at.at[pl.ds(WIDE - 6, 6)], o, after_group),
            push(at.at[pl.ds(WIDE, 6)], at.at[pl.ds(WIDE + GROUP, 6)], o, before_group),
        ]

    def halo(step, begin, count):
        ref = psi.at[step]
        far = begin + count
        return [
            push(
                ref.at[:, pl.ds(WIDE + GROUP - far, count)],
                ref.at[:, pl.ds(WIDE - far, count)],
                o,
                after_group,
            ),
            push(
                ref.at[:, pl.ds(WIDE + begin, count)],
                ref.at[:, pl.ds(WIDE + GROUP + begin, count)],
                o,
                before_group,
            ),
        ]

    def image(src, c, p, full):
        u = src[c, p]
        y_near, y_far = y_pairs(u, 2)
        near = (src[c, p - 1] + src[c, p + 1]) + (y_near + z_pair(u, 1))
        far = (src[c, p - 2] + src[c, p + 2]) + (y_far + z_pair(u, 2))
        return full * u - (2.0 / 3.0) * near + (1.0 / 24.0) * far

    def group_range(lo, hi, body):
        begin = jnp.maximum(lo, WIDE - GROUP * g)
        end = jnp.minimum(hi, WIDE + NX - GROUP * g)

        def run(p, carry):
            body(begin + 2 * p)
            body(begin + 2 * p + 1)
            return carry

        lax.fori_loop(0, (end - begin) // 2, run, 0)

    def term(step, order, lo, hi):
        src, dst = ((psi.at[step], t1), (t1, t2), (t2, t3), (t3, None))[order - 1]
        factor = TIME_STEP / order

        def body(p):
            full = pot[step, p] + 3.75
            re = factor * image(src, 1, p, full)
            im = -factor * image(src, 0, p, full)
            if order < TERMS:
                dst[0, p] = re
                dst[1, p] = im
                return
            re = re + (psi[step, 0, p] + t1[0, p]) + (t2[0, p] + t3[0, p])
            im = im + (psi[step, 1, p] + t1[1, p]) + (t2[1, p] + t3[1, p])
            if step == STEPS - 1:
                scatter(psi, re, step + 1, 0, p)
                scatter(psi, im, step + 1, 1, p)
            else:
                psi[step + 1, 0, p] = re
                psi[step + 1, 1, p] = im
                ringpart[p - WIDE] = weight(x) * (re * re + im * im)

        group_range(lo, hi, body)

    def inside(step):
        for order in range(1, TERMS + 1):
            cut = 2 * (order - 1)
            term(step, order, WIDE + cut, WIDE + GROUP - cut)

    def low_edge(step):
        for order in range(1, TERMS + 1):
            term(step, order, 2 * order, 2 * order + 6)

    def high_edge(step):
        for order in range(1, TERMS + 1):
            term(step, order, EXT - 6 - 2 * order, EXT - 2 * order)

    class Shares:
        def __init__(self, src_of, dst_of):
            self.copies = []
            for k in range(1, RING):
                to = mate(k)
                i = len(pending)
                copy = pltpu.make_async_remote_copy(
                    src_ref=src_of(to),
                    dst_ref=dst_of(k),
                    send_sem=send.at[i],
                    recv_sem=recv.at[i],
                    device_id={"orb": o, "dom": RING * g + to},
                    device_id_type=pl.DeviceIdType.MESH,
                )
                pending.append(copy)
                self.copies.append((to, copy))

        def begin(self, lo, hi):
            for to, copy in self.copies:
                pl.when(jnp.logical_and(to >= lo, to < hi))(copy.start)

        def wait(self):
            for unused, copy in self.copies:
                copy.wait_recv()

    regroup = []

    def begin_regroup():
        for k in range(1, RING):
            to = mate(k)
            regroup.append(
                push(psi_in.at[:, to], land.at[:, pl.ds(SLAB * x, SLAB)], o, RING * g + to)
            )

    halos = {}

    def regrouped():
        for copy in regroup:
            copy.wait_recv()
        own.wait()

        def reorder(p, carry):
            for c in range(2):
                psi[0, c, WIDE + p] = gathered(land, c, p)
            return carry

        lax.fori_loop(0, GROUP, reorder, 0)

    plans = (
        {"near": ("begin",), "source": ("end", (0, 2)), "again": ((2, 3),), "solved": ((5, 3),)},
        {"source": ((0, 2),), "again": ((2, 3),), "solved": ((5, 3),)},
    )

    def meanwhile(step, place):
        for what in plans[step].get(place, ()):
            if what == "begin":
                begin_regroup()
            elif what == "end":
                regrouped()
            else:
                halos[what] = halo(step, *what)

    def clear_outside(step, begin, count):
        @pl.when(g == 0)
        def _():
            clear_halo(WIDE - begin - count, count, (psi.at[step],))

        @pl.when(g == GROUPS - 1)
        def _():
            clear_halo(WIDE + GROUP + begin, count, (psi.at[step],))

    for step in range(STEPS):
        meanwhile(step, "start")
        solve(step, functools.partial(meanwhile, step))
        meanwhile(step, "solved")
        spread = spread_potential(step)
        meanwhile(step, "spread")
        for copy in spread:
            copy.wait_recv()
        spread = spread_halo(step)
        meanwhile(step, "beside")
        ready = [halos.pop(key) for key in sorted(halos)]
        for copy in ready[0]:
            copy.wait_recv()
        clear_outside(step, 0, 2)
        inside(step)
        for copy in sum(ready[1:], []):
            copy.wait_recv()
        clear_outside(step, 2, 6)
        for copy in spread:
            copy.wait_recv()
        later = psi.at[step + 1]
        if step < STEPS - 1:
            shares = Shares(
                lambda to: ringpart.at[pl.ds(SLAB * to, SLAB)],
                lambda k: ringpart.at[pl.ds(GROUP + SLAB * (k - 1), SLAB)],
            )
        else:
            shares = Shares(
                lambda to: later.at[:, pl.ds(WIDE + SLAB * to, SLAB)],
                lambda k: psi_out.at[:, x],
            )
        low_edge(step)
        shares.begin(0, RING // 2)
        high_edge(step)
        shares.begin(RING // 2, RING)
        if step < STEPS - 1:
            shares.wait()
            for p in range(SLAB):
                total = ringpart[SLAB * x + p]
                for k in range(1, RING):
                    total = total + ringpart[GROUP + SLAB * (k - 1) + p]
                part[step + 1, p] = total

    for p in range(SLAB):
        scatter(hartree_out, vb[WIDE + p], p)
    final = psi.at[STEPS]
    own = pltpu.make_async_copy(
        final.at[:, pl.ds(group_at, SLAB)], psi_out.at[:, x], local_sem.at[1]
    )
    own.start()
    shares.wait()
    own.wait()
    for copy in pending:
        copy.wait_send()


def per_device(orbitals, occupations, external, control):
    f32 = jnp.float32
    vmem = pl.BlockSpec(memory_space=pltpu.VMEM)
    smem = pl.BlockSpec(memory_space=pltpu.SMEM)
    fields = pltpu.VMEM((2, EXT, NY, NZ), f32)
    slab = pltpu.VMEM((STEPS, SLAB, NY, NZ), f32)
    slab_one = pltpu.VMEM((SLAB, NY, NZ), f32)
    mid = pltpu.VMEM((SLABS + 2, Y1, NZ), f32)
    low = pltpu.VMEM((SLABS + 2, Y2, NZ), f32)
    return pl.pallas_call(
        kernel,
        out_shape=(
            jax.ShapeDtypeStruct(orbitals.shape, f32),
            jax.ShapeDtypeStruct(external.shape, f32),
        ),
        in_specs=[vmem, smem, vmem, smem],
        out_specs=(pl.BlockSpec(memory_space=pl.ANY), vmem),
        scratch_shapes=[
            pltpu.VMEM((STEPS + 1, 2, EXT, NY, NZ), f32),
            fields, fields, fields,
            pltpu.VMEM((STEPS, EXT, NY, NZ), f32),
            slab,
            pltpu.VMEM((GROUP + SLAB * (RING - 1), NY, NZ), f32),
            slab, slab, slab,
            pltpu.VMEM((STEPS, FEXT, NY, NZ), f32),
            pltpu.VMEM((FEXT, NY, NZ), f32),
            pltpu.VMEM((FEXT, NY, NZ), f32),
            pltpu.VMEM((STEPS, 2, SLABS, 2, Y2, NZ), f32),
            mid, mid, low, low,
            pltpu.VMEM((SLABS, Y1, NZ), f32),
            pltpu.VMEM((SLABS, Y2, NZ), f32),
            pltpu.VMEM((2, GROUP, NY, NZ), f32),
            slab_one,
            pltpu.VMEM((SLABS, Y2, NZ), f32),
            pltpu.VMEM((10, NY, NZ), f32),
            pltpu.SemaphoreType.DMA((COPIES,)),
            pltpu.SemaphoreType.DMA((COPIES,)),
            pltpu.SemaphoreType.DMA((2,)),
        ],
        compiler_params=pltpu.CompilerParams(
            collective_id=0, has_side_effects=True, vmem_limit_bytes=56 * 1024 * 1024
        ),
    )(orbitals, occupations, external, control)


def solution(mesh):
    in_specs = (P(None, "orb", "dom", None, None), P("orb"), P("dom", None, None), P())
    out_specs = (P(None, "orb", "dom", None, None), P("dom", None, None))
    return jax.shard_map(
        per_device, mesh=mesh, in_specs=in_specs, out_specs=out_specs, check_vma=False
    )
```

```python
import functools

import jax
import jax.numpy as jnp
from jax import lax
from jax.experimental import pallas as pl
from jax.experimental.pallas import tpu as pltpu
from jax.sharding import PartitionSpec as P

STEPS = 2
TERMS = 4
TIME_STEP = 0.2
COUPLING = 0.025
RELAX = 0.8 / 6.0
KEEP = 0.2

ORB = 4
DOM = 64
RING = 4
GROUPS = DOM // RING
SLAB = 4
GROUP = RING * SLAB
WIDE = 8
NX = DOM * SLAB
NY, NZ = 64, 128
EXT = GROUP + 2 * WIDE
FEXT = SLAB + 2 * WIDE
REACH = 7
SLABS = 2 * REACH + 1
Y1, Y2 = NY // 2, NY // 4
COPIES = 160
HIGH = lax.Precision.HIGHEST


def dot(a, b):
    return jnp.dot(a, b, precision=HIGH, preferred_element_type=jnp.float32)


def iota(shape, dim):
    return lax.broadcasted_iota(jnp.int32, shape, dim)


def flipped(a, up):
    axis = a.ndim - 2
    place = iota(a.shape, axis)
    if up:
        return jnp.where(place <= 6, pltpu.roll(a, 7, axis), 0.0)
    return jnp.where(place >= 1, pltpu.roll(a, 1, axis), 0.0)


def rows(u, begin, count):
    return u[..., 8 * begin : 8 * (begin + count), :]


def y_pairs(u, reaches):
    tiles = u.shape[-2] // 8
    axis = u.ndim - 2
    first = [flipped(rows(u, i, 1), True) for i in range(reaches)]
    last = [flipped(rows(u, tiles - 1 - i, 1), False) for i in range(reaches)]
    sums = []
    for reach in range(1, reaches + 1):
        up = jnp.concatenate([rows(u, reach, tiles - reach)] + first[:reach], axis=axis)
        down = jnp.concatenate(last[:reach][::-1] + [rows(u, 0, tiles - reach)], axis=axis)
        sums.append(up + down)
    return sums


def z_pair(u, reach, period=NZ):
    axis = u.ndim - 1
    place = iota(u.shape, axis)
    if period < NZ:
        place = place % 64
    low = jnp.where(place >= reach, pltpu.roll(u, reach, axis), 0.0)
    high = jnp.where(place <= period - 1 - reach, pltpu.roll(u, NZ - reach, axis), 0.0)
    return low + high


def beside_fine(ref, p):
    u = ref[p]
    return u, (ref[p - 1] + ref[p + 1]) + (y_pairs(u, 1)[0] + z_pair(u, 1))


def beside_mid(ref):
    u = ref[1 : SLABS + 1]
    lane = iota(u.shape, 2)
    across = jnp.where(lane < 64, ref[2 : SLABS + 2], ref[0:SLABS])
    total = pltpu.roll(u + across, 64, 2)
    return u, total + (y_pairs(u, 1)[0] + z_pair(u, 1, 64))


def beside_low(ref):
    u = ref[1 : SLABS + 1]
    total = ref[2 : SLABS + 2] + ref[0:SLABS]
    return u, total + (y_pairs(u, 1)[0] + z_pair(u, 1, 32))


def halved(t):
    tiles = t.shape[-2] // 8
    pairs = [rows(t, 2 * i, 1) + rows(t, 2 * i + 1, 1) for i in range(tiles // 2)]
    return jnp.concatenate(pairs, axis=t.ndim - 2)


def doubled(t):
    tiles = t.shape[-2] // 8
    return jnp.concatenate([rows(t, i // 2, 1) for i in range(2 * tiles)], axis=t.ndim - 2)


def gathered(ref, *at):
    return jnp.concatenate([ref[(*at, pl.ds(v, 8, stride=8))] for v in range(8)], axis=0)


def scatter(ref, value, *at):
    for v in range(8):
        ref[(*at, pl.ds(v, 8, stride=8))] = value[8 * v : 8 * v + 8]


def kernel(
    psi_in, occ, ext, control, psi_out, hartree_out,
    psi, t1, t2, t3, pot, part, ringpart, half, d1, d2, f, va, vb, c1, m_a, m_b, l_a, l_b, mask1, mask2,
    land, plane, tmp_low, up, send, recv, local_sem,
):
    o = lax.axis_index("orb")
    d = lax.axis_index("dom")
    x = lax.rem(d, RING)
    g = lax.div(d, RING)

    barrier = pltpu.get_barrier_semaphore()
    for k in range(1, REACH + 1):
        for to in (lax.rem(d + k, DOM), lax.rem(d + DOM - k, DOM)):
            pl.semaphore_signal(barrier, inc=1, device_id={"orb": o, "dom": to})
    for k in range(1, ORB):
        pl.semaphore_signal(barrier, inc=1, device_id={"orb": lax.rem(o + k, ORB), "dom": d})

    own = pltpu.make_async_copy(
        psi_in.at[:, x], land.at[:, pl.ds(SLAB * x, SLAB)], local_sem.at[0]
    )
    own.start()

    def weight(b):
        return occ[b].astype(jnp.float32) * (1.0 / 16.0)

    for p in range(SLAB):
        total = jnp.zeros((NY, NZ), jnp.float32)
        for b in range(4):
            re, im = psi_in[0, b, p], psi_in[1, b, p]
            total = total + weight(b) * (re * re + im * im)
        plane[p] = total
        part[0, p] = gathered(plane, p)

    for s in range(SLABS):
        inside = jnp.logical_and(d - REACH + s >= 0, d - REACH + s < DOM)
        factor = jnp.where(inside, 1.0, 0.0).astype(jnp.float32)
        mask1[s] = jnp.full((Y1, NZ), 1.0, jnp.float32) * factor
        mask2[s] = jnp.full((Y2, NZ), 1.0, jnp.float32) * factor
    for ref in (m_a, m_b, l_a, l_b):
        ref[0] = jnp.zeros(ref.shape[1:], jnp.float32)
        ref[SLABS + 1] = jnp.zeros(ref.shape[1:], jnp.float32)

    def clear_fine(p, carry):
        va[p] = jnp.zeros((NY, NZ), jnp.float32)
        vb[p] = jnp.zeros((NY, NZ), jnp.float32)
        return carry

    lax.fori_loop(0, FEXT, clear_fine, 0)

    def clear_halo(begin, count, refs):
        def body(p, carry):
            for ref in refs:
                for c in range(2):
                    ref[c, p] = jnp.zeros((NY, NZ), jnp.float32)
            return carry

        lax.fori_loop(begin, begin + count, body, 0)

    @pl.when(g == 0)
    def _():
        clear_halo(0, WIDE, (t1, t2, t3))

    @pl.when(g == GROUPS - 1)
    def _():
        clear_halo(WIDE + GROUP, WIDE, (t1, t2, t3))

    pl.semaphore_wait(barrier, 2 * REACH + ORB - 1)

    pending = []

    def push(src, dst, orb, dom):
        i = len(pending)
        copy = pltpu.make_async_remote_copy(
            src_ref=src,
            dst_ref=dst,
            send_sem=send.at[i],
            recv_sem=recv.at[i],
            device_id={"orb": orb, "dom": dom},
            device_id_type=pl.DeviceIdType.MESH,
        )
        copy.start()
        pending.append(copy)
        return copy

    def mate(k):
        return lax.rem(x + k, RING)

    after_group, before_group = lax.rem(d + RING, DOM), lax.rem(d + DOM - RING, DOM)
    group_at = WIDE + SLAB * x
    core = lax.rem(o, 2)
    sibling = o + 1 - 2 * core

    row, col = iota((2 * NZ, NZ), 0), iota((2 * NZ, NZ), 1)
    down_fine = jnp.where(row // 2 == col, 0.125, 0.0).astype(jnp.float32)
    row, col = iota((NZ, NZ), 0), iota((NZ, NZ), 1)
    down_mid = jnp.where((row % 64) // 2 == col, 0.125, 0.0).astype(jnp.float32)
    up_low = jnp.where(row == (col % 64) // 2, 1.0, 0.0).astype(jnp.float32)
    row, col = iota((NZ, 2 * NZ), 0), iota((NZ, 2 * NZ), 1)
    up_mid = jnp.where(row == col // 2, 1.0, 0.0).astype(jnp.float32)

    def fine_range(lo, hi, body):
        begin = jnp.maximum(lo, WIDE - SLAB * d)
        end = jnp.minimum(hi, WIDE + NX - SLAB * d)

        def run(p, carry):
            body(p)
            return carry

        lax.fori_loop(begin, end, run, 0)

    def sweep_fine(step, src, dst, lo, hi):
        def body(p):
            u, beside = beside_fine(src, p)
            dst[p] = KEEP * u + RELAX * (f[step, p] + beside)

        fine_range(lo, hi, body)

    def coarse_source(step, cycle, v):
        sides = []
        for pair in range(2):
            total = None
            for p in (WIDE + 2 * pair, WIDE + 2 * pair + 1):
                u, beside = beside_fine(v, p)
                r = f[step, p] - (6.0 * u - beside)
                total = r if total is None else total + r
            sides.append(halved(total))
        c1[step, cycle, REACH] = dot(jnp.concatenate(sides, axis=1), down_fine).reshape(2, Y2, NZ)
        copies = []
        reach = REACH if cycle == 0 else REACH - 1
        for k in range(1, reach + 1):
            src = c1.at[step, cycle, REACH]
            low = c1.at[step, cycle, REACH - k]
            high = c1.at[step, cycle, REACH + k]
            copies.append(push(src, low, o, lax.rem(d + k, DOM)))
            copies.append(push(src, high, o, lax.rem(d + DOM - k, DOM)))
        return copies

    def whole_source(step, cycle, copies):
        for copy in copies:
            copy.wait_recv()

    def coarse_solve(step, cycle, lo, hi):
        if cycle == 1:
            c1[step, cycle, 0] = jnp.zeros((2, Y2, NZ), jnp.float32)
            c1[step, cycle, SLABS - 1] = jnp.zeros((2, Y2, NZ), jnp.float32)
        mid = slice(1, SLABS + 1)

        def source():
            return c1[step, cycle].reshape(SLABS, Y1, NZ)

        def sweep(src, dst):
            u, beside = beside_mid(src)
            dst[mid] = (KEEP * u + RELAX * (4.0 * source() + beside)) * mask1[...]

        m_a[mid] = (4.0 * RELAX) * source() * mask1[...]
        sweep(m_a, m_b)
        u, beside = beside_mid(m_b)
        r = source() - 0.25 * (6.0 * u - beside)
        low = dot(halved(r).reshape(SLABS * Y2, NZ), down_mid)
        tmp_low[...] = low.reshape(SLABS, Y2, NZ)
        l_a[mid] = (16.0 * RELAX) * tmp_low[...] * mask2[...]
        src, dst = l_a, l_b
        for unused in range(3):
            u, beside = beside_low(src)
            dst[mid] = (KEEP * u + RELAX * (16.0 * tmp_low[...] + beside)) * mask2[...]
            src, dst = dst, src
        wide = dot(src[mid].reshape(SLABS * Y2, NZ), up_low)
        m_a[mid] = m_b[mid] + doubled(wide.reshape(SLABS, Y2, NZ))
        sweep(m_a, m_b)
        sweep(m_b, m_a)
        count = hi - lo
        fine = dot(m_a[1 + lo : 1 + hi].reshape(count * Y1, NZ), up_mid)
        for j in range(count):
            for side in range(2):
                piece = fine[j * Y1 : (j + 1) * Y1, side * NZ : (side + 1) * NZ]
                up[2 * j + side] = doubled(piece)

    def add_up(v, lo, hi, base):
        def body(p):
            v[p] = v[p] + up[(p - base) // 2]

        fine_range(lo, hi, body)

    def solve(step, meanwhile):
        swap = push(part.at[step], d1.at[step], sibling, d)
        swap.wait_recv()
        for p in range(SLAB):
            half[step, p] = part[step, p] + d1[step, p]
        swap = push(half.at[step], d2.at[step], lax.rem(o + 2, ORB), d)
        swap.wait_recv()
        for p in range(SLAB):
            f[step, WIDE + p] = COUPLING * (half[step, p] + d2[step, p])

        meanwhile('density')
        after = [lax.rem(d + k, DOM) for k in (1, 2)]
        before = [lax.rem(d + DOM - k, DOM) for k in (1, 2)]
        fs = f.at[step]
        near = [
            push(fs.at[pl.ds(WIDE + 2, 2)], fs.at[pl.ds(WIDE - 2, 2)], o, after[0]),
            push(fs.at[pl.ds(WIDE, 2)], fs.at[pl.ds(WIDE + SLAB, 2)], o, before[0]),
        ]
        far = [
            push(fs.at[pl.ds(WIDE + core, 1)], fs.at[pl.ds(WIDE - 4 + core, 1)], o, after[0]),
            push(fs.at[pl.ds(WIDE + 2 + core, 1)], fs.at[pl.ds(14 + core, 1)], o, before[0]),
            push(fs.at[pl.ds(WIDE + 2 * core, 2)], fs.at[pl.ds(2 * core, 2)], o, after[1]),
            push(fs.at[pl.ds(WIDE + 2 * core, 2)], fs.at[pl.ds(16 + 2 * core, 2)], o, before[1]),
        ]

        meanwhile('near')

        def first(lo, hi):
            def body(p):
                va[p] = RELAX * f[step, p]

            fine_range(lo, hi, body)

        for copy in near:
            copy.wait_recv()
        first(6, 14)
        sweep_fine(step, va, vb, 7, 13)
        copies = coarse_source(step, 0, vb)
        meanwhile('source')
        for copy in far:
            copy.wait_recv()
        far = []
        for at, count in ((4 + core, 1), (14 + core, 1), (2 * core, 2), (16 + 2 * core, 2)):
            piece = fs.at[pl.ds(at, count)]
            far.append(push(piece, piece, sibling, d))
        for copy in far:
            copy.wait_recv()
        first(1, 6)
        first(14, 19)
        sweep_fine(step, va, vb, 2, 7)
        sweep_fine(step, va, vb, 13, 18)
        whole_source(step, 0, copies)
        coarse_solve(step, 0, REACH - 2, REACH + 3)
        add_up(vb, 2, 18, 0)
        sweep_fine(step, vb, va, 3, 17)
        sweep_fine(step, va, vb, 4, 16)
        sweep_fine(step, vb, va, 5, 15)
        sweep_fine(step, va, vb, 6, 14)
        copies = coarse_source(step, 1, vb)
        meanwhile('again')
        whole_source(step, 1, copies)
        meanwhile('whole')
        coarse_solve(step, 1, REACH - 1, REACH + 2)
        add_up(vb, 6, 14, 4)
        sweep_fine(step, vb, va, 7, 13)
        sweep_fine(step, va, vb, 8, 12)

    def spread_potential(step):
        for p in range(SLAB):
            place = (SLAB * d + p).astype(jnp.float32)
            dipole = (place + 0.5) * (2.0 / NX) - 1.0
            pot[step, group_at + p] = gathered(ext, p) + vb[WIDE + p] + control[step] * dipole
        src = pot.at[step, pl.ds(group_at + 2 * core, 2)]
        return [push(src, src, o, RING * g + mate(k)) for k in range(1, RING)]

    def swap_potential(step):
        pieces = [pot.at[step, pl.ds(WIDE + SLAB * mate(k) + 2 * core, 2)] for k in range(1, RING)]
        return [push(piece, piece, sibling, d) for piece in pieces]

    def spread_halo(step):
        at = pot.at[step]
        return [
            push(at.at[pl.ds(WIDE + GROUP - 6 + 3 * core, 3)], at.at[pl.ds(WIDE - 6 + 3 * core, 3)], o, after_group),
            push(at.at[pl.ds(WIDE + 3 * core, 3)], at.at[pl.ds(WIDE + GROUP + 3 * core, 3)], o, before_group),
        ]

    def swap_halo(step):
        at = pot.at[step]
        pieces = [at.at[pl.ds(WIDE - 6 + 3 * core, 3)], at.at[pl.ds(WIDE + GROUP + 3 * core, 3)]]
        return [push(piece, piece, sibling, d) for piece in pieces]

    def halo(step, begin, count):
        ref = psi.at[step]
        far = begin + count
        return [
            push(
                ref.at[:, pl.ds(WIDE + GROUP - far, count)],
                ref.at[:, pl.ds(WIDE - far, count)],
                o,
                after_group,
            ),
            push(
                ref.at[:, pl.ds(WIDE + begin, count)],
                ref.at[:, pl.ds(WIDE + GROUP + begin, count)],
                o,
                before_group,
            ),
        ]

    def image(src, c, p, full):
        u = src[c, p]
        y_near, y_far = y_pairs(u, 2)
        near = (src[c, p - 1] + src[c, p + 1]) + (y_near + z_pair(u, 1))
        far = (src[c, p - 2] + src[c, p + 2]) + (y_far + z_pair(u, 2))
        return full * u - (2.0 / 3.0) * near + (1.0 / 24.0) * far

    def group_range(lo, hi, body):
        begin = jnp.maximum(lo, WIDE - GROUP * g)
        end = jnp.minimum(hi, WIDE + NX - GROUP * g)

        def run(p, carry):
            body(begin + 2 * p)
            body(begin + 2 * p + 1)
            return carry

        lax.fori_loop(0, (end - begin) // 2, run, 0)

    def term(step, order, lo, hi):
        src, dst = ((psi.at[step], t1), (t1, t2), (t2, t3), (t3, None))[order - 1]
        factor = TIME_STEP / order

        def body(p):
            full = pot[step, p] + 3.75
            re = factor * image(src, 1, p, full)
            im = -factor * image(src, 0, p, full)
            if order < TERMS:
                dst[0, p] = re
                dst[1, p] = im
                return
            re = re + (psi[step, 0, p] + t1[0, p]) + (t2[0, p] + t3[0, p])
            im = im + (psi[step, 1, p] + t1[1, p]) + (t2[1, p] + t3[1, p])
            if step == STEPS - 1:
                scatter(psi, re, step + 1, 0, p)
                scatter(psi, im, step + 1, 1, p)
            else:
                psi[step + 1, 0, p] = re
                psi[step + 1, 1, p] = im
                ringpart[p - WIDE] = weight(x) * (re * re + im * im)

        group_range(lo, hi, body)

    def inside(step):
        for order in range(1, TERMS + 1):
            cut = 2 * (order - 1)
            term(step, order, WIDE + cut, WIDE + GROUP - cut)

    def low_edge(step):
        for order in range(1, TERMS + 1):
            term(step, order, 2 * order, 2 * order + 6)

    def high_edge(step):
        for order in range(1, TERMS + 1):
            term(step, order, EXT - 6 - 2 * order, EXT - 2 * order)

    class Shares:
        def __init__(self, src_of, dst_of):
            self.copies = []
            for k in range(1, RING):
                to = mate(k)
                i = len(pending)
                copy = pltpu.make_async_remote_copy(
                    src_ref=src_of(to),
                    dst_ref=dst_of(k),
                    send_sem=send.at[i],
                    recv_sem=recv.at[i],
                    device_id={"orb": o, "dom": RING * g + to},
                    device_id_type=pl.DeviceIdType.MESH,
                )
                pending.append(copy)
                self.copies.append((to, copy))

        def begin(self, lo, hi):
            for to, copy in self.copies:
                pl.when(jnp.logical_and(to >= lo, to < hi))(copy.start)

        def wait(self):
            for unused, copy in self.copies:
                copy.wait_recv()

    regroup = []

    def begin_regroup():
        for k in range(1, RING):
            to = mate(k)
            regroup.append(
                push(psi_in.at[:, to], land.at[:, pl.ds(SLAB * x, SLAB)], o, RING * g + to)
            )

    halos = {}

    def regrouped():
        for copy in regroup:
            copy.wait_recv()
        own.wait()

        def reorder(p, carry):
            for c in range(2):
                psi[0, c, WIDE + p] = gathered(land, c, p)
            return carry

        lax.fori_loop(0, GROUP, reorder, 0)

    plans = (
        {'near': ('begin',), 'source': ('end', (0, 2)), 'again': ((2, 2),), 'solved': ((4, 4),)},
        {'source': ((0, 2),), 'again': ((2, 2),), 'solved': ((4, 4),)},
    )

    def meanwhile(step, place):
        for what in plans[step].get(place, ()):
            if what == "begin":
                begin_regroup()
            elif what == "end":
                regrouped()
            else:
                halos[what] = halo(step, *what)

    def clear_outside(step, begin, count):
        @pl.when(g == 0)
        def _():
            clear_halo(WIDE - begin - count, count, (psi.at[step],))

        @pl.when(g == GROUPS - 1)
        def _():
            clear_halo(WIDE + GROUP + begin, count, (psi.at[step],))

    for step in range(STEPS):
        meanwhile(step, "start")
        solve(step, functools.partial(meanwhile, step))
        meanwhile(step, "solved")
        spread = spread_potential(step)
        meanwhile(step, "spread")
        for copy in spread:
            copy.wait_recv()
        for copy in swap_potential(step):
            copy.wait_recv()
        spread = spread_halo(step)
        meanwhile(step, "beside")
        ready = [halos.pop(key) for key in sorted(halos)]
        for copy in ready[0]:
            copy.wait_recv()
        clear_outside(step, 0, 2)
        inside(step)
        for copy in sum(ready[1:], []):
            copy.wait_recv()
        clear_outside(step, 2, 6)
        for copy in spread:
            copy.wait_recv()
        for copy in swap_halo(step):
            copy.wait_recv()
        later = psi.at[step + 1]
        if step < STEPS - 1:
            shares = Shares(
                lambda to: ringpart.at[pl.ds(SLAB * to, SLAB)],
                lambda k: ringpart.at[pl.ds(GROUP + SLAB * (k - 1), SLAB)],
            )
        else:
            shares = Shares(
                lambda to: later.at[:, pl.ds(WIDE + SLAB * to, SLAB)],
                lambda k: psi_out.at[:, x],
            )
        low_edge(step)
        shares.begin(0, RING // 2)
        high_edge(step)
        shares.begin(RING // 2, RING)
        if step < STEPS - 1:
            shares.wait()
            for p in range(SLAB):
                total = ringpart[SLAB * x + p]
                for k in range(1, RING):
                    total = total + ringpart[GROUP + SLAB * (k - 1) + p]
                part[step + 1, p] = total

    for p in range(SLAB):
        scatter(hartree_out, vb[WIDE + p], p)
    final = psi.at[STEPS]
    own = pltpu.make_async_copy(
        final.at[:, pl.ds(group_at, SLAB)], psi_out.at[:, x], local_sem.at[1]
    )
    own.start()
    shares.wait()
    own.wait()
    for copy in pending:
        copy.wait_send()


def per_device(orbitals, occupations, external, control):
    f32 = jnp.float32
    vmem = pl.BlockSpec(memory_space=pltpu.VMEM)
    smem = pl.BlockSpec(memory_space=pltpu.SMEM)
    fields = pltpu.VMEM((2, EXT, NY, NZ), f32)
    slab = pltpu.VMEM((STEPS, SLAB, NY, NZ), f32)
    slab_one = pltpu.VMEM((SLAB, NY, NZ), f32)
    mid = pltpu.VMEM((SLABS + 2, Y1, NZ), f32)
    low = pltpu.VMEM((SLABS + 2, Y2, NZ), f32)
    return pl.pallas_call(
        kernel,
        out_shape=(
            jax.ShapeDtypeStruct(orbitals.shape, f32),
            jax.ShapeDtypeStruct(external.shape, f32),
        ),
        in_specs=[vmem, smem, vmem, smem],
        out_specs=(pl.BlockSpec(memory_space=pl.ANY), vmem),
        scratch_shapes=[
            pltpu.VMEM((STEPS + 1, 2, EXT, NY, NZ), f32),
            fields, fields, fields,
            pltpu.VMEM((STEPS, EXT, NY, NZ), f32),
            slab,
            pltpu.VMEM((GROUP + SLAB * (RING - 1), NY, NZ), f32),
            slab, slab, slab,
            pltpu.VMEM((STEPS, FEXT, NY, NZ), f32),
            pltpu.VMEM((FEXT, NY, NZ), f32),
            pltpu.VMEM((FEXT, NY, NZ), f32),
            pltpu.VMEM((STEPS, 2, SLABS, 2, Y2, NZ), f32),
            mid, mid, low, low,
            pltpu.VMEM((SLABS, Y1, NZ), f32),
            pltpu.VMEM((SLABS, Y2, NZ), f32),
            pltpu.VMEM((2, GROUP, NY, NZ), f32),
            slab_one,
            pltpu.VMEM((SLABS, Y2, NZ), f32),
            pltpu.VMEM((10, NY, NZ), f32),
            pltpu.SemaphoreType.DMA((COPIES,)),
            pltpu.SemaphoreType.DMA((COPIES,)),
            pltpu.SemaphoreType.DMA((2,)),
        ],
        compiler_params=pltpu.CompilerParams(
            collective_id=0, has_side_effects=True, vmem_limit_bytes=56 * 1024 * 1024
        ),
    )(orbitals, occupations, external, control)


def solution(mesh):
    in_specs = (P(None, "orb", "dom", None, None), P("orb"), P("dom", None, None), P())
    out_specs = (P(None, "orb", "dom", None, None), P("dom", None, None))
    return jax.shard_map(
        per_device, mesh=mesh, in_specs=in_specs, out_specs=out_specs, check_vma=False
    )
```

```python
import functools

import jax
import jax.numpy as jnp
from jax import lax
from jax.experimental import pallas as pl
from jax.experimental.pallas import tpu as pltpu
from jax.sharding import PartitionSpec as P

STEPS = 2
TERMS = 4
TIME_STEP = 0.2
COUPLING = 0.025
RELAX = 0.8 / 6.0
KEEP = 0.2

ORB = 4
DOM = 64
RING = 4
GROUPS = DOM // RING
SLAB = 4
GROUP = RING * SLAB
WIDE = 8
NX = DOM * SLAB
NY, NZ = 64, 128
EXT = GROUP + 2 * WIDE
FEXT = SLAB + 2 * WIDE
REACH = 7
SLABS = 2 * REACH + 1
Y1, Y2 = NY // 2, NY // 4
COPIES = 160
HIGH = lax.Precision.HIGHEST


def dot(a, b):
    return jnp.dot(a, b, precision=HIGH, preferred_element_type=jnp.float32)


def iota(shape, dim):
    return lax.broadcasted_iota(jnp.int32, shape, dim)


def flipped(a, up):
    axis = a.ndim - 2
    place = iota(a.shape, axis)
    if up:
        return jnp.where(place <= 6, pltpu.roll(a, 7, axis), 0.0)
    return jnp.where(place >= 1, pltpu.roll(a, 1, axis), 0.0)


def rows(u, begin, count):
    return u[..., 8 * begin : 8 * (begin + count), :]


def y_pairs(u, reaches):
    tiles = u.shape[-2] // 8
    axis = u.ndim - 2
    first = [flipped(rows(u, i, 1), True) for i in range(reaches)]
    last = [flipped(rows(u, tiles - 1 - i, 1), False) for i in range(reaches)]
    sums = []
    for reach in range(1, reaches + 1):
        up = jnp.concatenate([rows(u, reach, tiles - reach)] + first[:reach], axis=axis)
        down = jnp.concatenate(last[:reach][::-1] + [rows(u, 0, tiles - reach)], axis=axis)
        sums.append(up + down)
    return sums


def z_pair(u, reach, period=NZ):
    axis = u.ndim - 1
    place = iota(u.shape, axis)
    if period < NZ:
        place = place % 64
    low = jnp.where(place >= reach, pltpu.roll(u, reach, axis), 0.0)
    high = jnp.where(place <= period - 1 - reach, pltpu.roll(u, NZ - reach, axis), 0.0)
    return low + high


def beside_fine(ref, p):
    u = ref[p]
    return u, (ref[p - 1] + ref[p + 1]) + (y_pairs(u, 1)[0] + z_pair(u, 1))


def beside_mid(ref):
    u = ref[1 : SLABS + 1]
    lane = iota(u.shape, 2)
    across = jnp.where(lane < 64, ref[2 : SLABS + 2], ref[0:SLABS])
    total = pltpu.roll(u + across, 64, 2)
    return u, total + (y_pairs(u, 1)[0] + z_pair(u, 1, 64))


def beside_low(ref):
    u = ref[1 : SLABS + 1]
    total = ref[2 : SLABS + 2] + ref[0:SLABS]
    return u, total + (y_pairs(u, 1)[0] + z_pair(u, 1, 32))


def halved(t):
    tiles = t.shape[-2] // 8
    pairs = [rows(t, 2 * i, 1) + rows(t, 2 * i + 1, 1) for i in range(tiles // 2)]
    return jnp.concatenate(pairs, axis=t.ndim - 2)


def doubled(t):
    tiles = t.shape[-2] // 8
    return jnp.concatenate([rows(t, i // 2, 1) for i in range(2 * tiles)], axis=t.ndim - 2)


def gathered(ref, *at):
    return jnp.concatenate([ref[(*at, pl.ds(v, 8, stride=8))] for v in range(8)], axis=0)


def scatter(ref, value, *at):
    for v in range(8):
        ref[(*at, pl.ds(v, 8, stride=8))] = value[8 * v : 8 * v + 8]


def kernel(
    psi_in, occ, ext, control, psi_out, hartree_out,
    psi, t1, t2, t3, pot, part, ringpart, half, d1, d2, f, va, vb, c1, m_a, m_b, l_a, l_b, mask1, mask2,
    land, plane, tmp_low, up, send, recv, local_sem,
):
    o = lax.axis_index("orb")
    d = lax.axis_index("dom")
    x = lax.rem(d, RING)
    g = lax.div(d, RING)

    barrier = pltpu.get_barrier_semaphore()
    for k in range(1, REACH + 1):
        for to in (lax.rem(d + k, DOM), lax.rem(d + DOM - k, DOM)):
            pl.semaphore_signal(barrier, inc=1, device_id={"orb": o, "dom": to})
    for k in range(1, ORB):
        pl.semaphore_signal(barrier, inc=1, device_id={"orb": lax.rem(o + k, ORB), "dom": d})

    own = pltpu.make_async_copy(
        psi_in.at[:, x], land.at[:, pl.ds(SLAB * x, SLAB)], local_sem.at[0]
    )
    own.start()

    def weight(b):
        return occ[b].astype(jnp.float32) * (1.0 / 16.0)

    for p in range(SLAB):
        total = jnp.zeros((NY, NZ), jnp.float32)
        for b in range(4):
            re, im = psi_in[0, b, p], psi_in[1, b, p]
            total = total + weight(b) * (re * re + im * im)
        plane[p] = total
        part[0, p] = gathered(plane, p)

    for s in range(SLABS):
        inside = jnp.logical_and(d - REACH + s >= 0, d - REACH + s < DOM)
        factor = jnp.where(inside, 1.0, 0.0).astype(jnp.float32)
        mask1[s] = jnp.full((Y1, NZ), 1.0, jnp.float32) * factor
        mask2[s] = jnp.full((Y2, NZ), 1.0, jnp.float32) * factor
    for ref in (m_a, m_b, l_a, l_b):
        ref[0] = jnp.zeros(ref.shape[1:], jnp.float32)
        ref[SLABS + 1] = jnp.zeros(ref.shape[1:], jnp.float32)

    def clear_fine(p, carry):
        va[p] = jnp.zeros((NY, NZ), jnp.float32)
        vb[p] = jnp.zeros((NY, NZ), jnp.float32)
        return carry

    lax.fori_loop(0, FEXT, clear_fine, 0)

    def clear_halo(begin, count, refs):
        def body(p, carry):
            for ref in refs:
                for c in range(2):
                    ref[c, p] = jnp.zeros((NY, NZ), jnp.float32)
            return carry

        lax.fori_loop(begin, begin + count, body, 0)

    @pl.when(g == 0)
    def _():
        clear_halo(0, WIDE, (t1, t2, t3))

    @pl.when(g == GROUPS - 1)
    def _():
        clear_halo(WIDE + GROUP, WIDE, (t1, t2, t3))

    pl.semaphore_wait(barrier, 2 * REACH + ORB - 1)

    pending = []

    def push(src, dst, orb, dom):
        i = len(pending)
        copy = pltpu.make_async_remote_copy(
            src_ref=src,
            dst_ref=dst,
            send_sem=send.at[i],
            recv_sem=recv.at[i],
            device_id={"orb": orb, "dom": dom},
            device_id_type=pl.DeviceIdType.MESH,
        )
        copy.start()
        pending.append(copy)
        return copy

    def mate(k):
        return lax.rem(x + k, RING)

    after_group, before_group = lax.rem(d + RING, DOM), lax.rem(d + DOM - RING, DOM)
    group_at = WIDE + SLAB * x
    core = lax.rem(o, 2)
    sibling = o + 1 - 2 * core

    row, col = iota((2 * NZ, NZ), 0), iota((2 * NZ, NZ), 1)
    down_fine = jnp.where(row // 2 == col, 0.125, 0.0).astype(jnp.float32)
    row, col = iota((NZ, NZ), 0), iota((NZ, NZ), 1)
    down_mid = jnp.where((row % 64) // 2 == col, 0.125, 0.0).astype(jnp.float32)
    up_low = jnp.where(row == (col % 64) // 2, 1.0, 0.0).astype(jnp.float32)
    row, col = iota((NZ, 2 * NZ), 0), iota((NZ, 2 * NZ), 1)
    up_mid = jnp.where(row == col // 2, 1.0, 0.0).astype(jnp.float32)

    def fine_range(lo, hi, body):
        begin = jnp.maximum(lo, WIDE - SLAB * d)
        end = jnp.minimum(hi, WIDE + NX - SLAB * d)

        def run(p, carry):
            body(p)
            return carry

        lax.fori_loop(begin, end, run, 0)

    def sweep_fine(step, src, dst, lo, hi):
        def body(p):
            u, beside = beside_fine(src, p)
            dst[p] = KEEP * u + RELAX * (f[step, p] + beside)

        fine_range(lo, hi, body)

    def coarse_source(step, cycle, v):
        sides = []
        for pair in range(2):
            total = None
            for p in (WIDE + 2 * pair, WIDE + 2 * pair + 1):
                u, beside = beside_fine(v, p)
                r = f[step, p] - (6.0 * u - beside)
                total = r if total is None else total + r
            sides.append(halved(total))
        c1[step, cycle, REACH] = dot(jnp.concatenate(sides, axis=1), down_fine).reshape(2, Y2, NZ)
        copies = []
        reach = REACH if cycle == 0 else REACH - 1
        for k in range(1, reach + 1):
            src = c1.at[step, cycle, REACH]
            low = c1.at[step, cycle, REACH - k]
            high = c1.at[step, cycle, REACH + k]
            copies.append(push(src, low, o, lax.rem(d + k, DOM)))
            copies.append(push(src, high, o, lax.rem(d + DOM - k, DOM)))
        return copies

    def whole_source(step, cycle, copies):
        for copy in copies:
            copy.wait_recv()

    def coarse_solve(step, cycle, lo, hi):
        if cycle == 1:
            c1[step, cycle, 0] = jnp.zeros((2, Y2, NZ), jnp.float32)
            c1[step, cycle, SLABS - 1] = jnp.zeros((2, Y2, NZ), jnp.float32)
        mid = slice(1, SLABS + 1)

        def source():
            return c1[step, cycle].reshape(SLABS, Y1, NZ)

        def sweep(src, dst):
            u, beside = beside_mid(src)
            dst[mid] = (KEEP * u + RELAX * (4.0 * source() + beside)) * mask1[...]

        m_a[mid] = (4.0 * RELAX) * source() * mask1[...]
        sweep(m_a, m_b)
        u, beside = beside_mid(m_b)
        r = source() - 0.25 * (6.0 * u - beside)
        low = dot(halved(r).reshape(SLABS * Y2, NZ), down_mid)
        tmp_low[...] = low.reshape(SLABS, Y2, NZ)
        l_a[mid] = (16.0 * RELAX) * tmp_low[...] * mask2[...]
        src, dst = l_a, l_b
        for unused in range(3):
            u, beside = beside_low(src)
            dst[mid] = (KEEP * u + RELAX * (16.0 * tmp_low[...] + beside)) * mask2[...]
            src, dst = dst, src
        wide = dot(src[mid].reshape(SLABS * Y2, NZ), up_low)
        m_a[mid] = m_b[mid] + doubled(wide.reshape(SLABS, Y2, NZ))
        sweep(m_a, m_b)
        sweep(m_b, m_a)
        count = hi - lo
        fine = dot(m_a[1 + lo : 1 + hi].reshape(count * Y1, NZ), up_mid)
        for j in range(count):
            for side in range(2):
                piece = fine[j * Y1 : (j + 1) * Y1, side * NZ : (side + 1) * NZ]
                up[2 * j + side] = doubled(piece)

    def add_up(v, lo, hi, base):
        def body(p):
            v[p] = v[p] + up[(p - base) // 2]

        fine_range(lo, hi, body)

    def solve(step, meanwhile):
        swap = push(part.at[step], d1.at[step], sibling, d)
        swap.wait_recv()
        for p in range(SLAB):
            half[step, p] = part[step, p] + d1[step, p]
        swap = push(half.at[step], d2.at[step], lax.rem(o + 2, ORB), d)
        swap.wait_recv()
        for p in range(SLAB):
            f[step, WIDE + p] = COUPLING * (half[step, p] + d2[step, p])

        meanwhile('density')
        after = [lax.rem(d + k, DOM) for k in (1, 2)]
        before = [lax.rem(d + DOM - k, DOM) for k in (1, 2)]
        fs = f.at[step]
        near = [
            push(fs.at[pl.ds(WIDE + 2, 2)], fs.at[pl.ds(WIDE - 2, 2)], o, after[0]),
            push(fs.at[pl.ds(WIDE, 2)], fs.at[pl.ds(WIDE + SLAB, 2)], o, before[0]),
        ]
        far = [
            push(fs.at[pl.ds(WIDE + core, 1)], fs.at[pl.ds(WIDE - 4 + core, 1)], o, after[0]),
            push(fs.at[pl.ds(WIDE + 2 + core, 1)], fs.at[pl.ds(14 + core, 1)], o, before[0]),
            push(fs.at[pl.ds(WIDE + 2 * core, 2)], fs.at[pl.ds(2 * core, 2)], o, after[1]),
            push(fs.at[pl.ds(WIDE + 2 * core, 2)], fs.at[pl.ds(16 + 2 * core, 2)], o, before[1]),
        ]

        meanwhile('near')

        def first(lo, hi):
            def body(p):
                va[p] = RELAX * f[step, p]

            fine_range(lo, hi, body)

        for copy in near:
            copy.wait_recv()
        first(6, 14)
        sweep_fine(step, va, vb, 7, 13)
        copies = coarse_source(step, 0, vb)
        meanwhile('source')
        for copy in far:
            copy.wait_recv()
        far = []
        for at, count in ((4 + core, 1), (14 + core, 1), (2 * core, 2), (16 + 2 * core, 2)):
            piece = fs.at[pl.ds(at, count)]
            far.append(push(piece, piece, sibling, d))
        for copy in far:
            copy.wait_recv()
        first(1, 6)
        first(14, 19)
        sweep_fine(step, va, vb, 2, 7)
        sweep_fine(step, va, vb, 13, 18)
        whole_source(step, 0, copies)
        coarse_solve(step, 0, REACH - 2, REACH + 3)
        add_up(vb, 2, 18, 0)
        sweep_fine(step, vb, va, 3, 17)
        sweep_fine(step, va, vb, 4, 16)
        sweep_fine(step, vb, va, 5, 15)
        sweep_fine(step, va, vb, 6, 14)
        copies = coarse_source(step, 1, vb)
        meanwhile('again')
        whole_source(step, 1, copies)
        meanwhile('whole')
        coarse_solve(step, 1, REACH - 1, REACH + 2)
        add_up(vb, 6, 14, 4)
        sweep_fine(step, vb, va, 7, 13)
        sweep_fine(step, va, vb, 8, 12)

    def spread_potential(step):
        for p in range(SLAB):
            place = (SLAB * d + p).astype(jnp.float32)
            dipole = (place + 0.5) * (2.0 / NX) - 1.0
            pot[step, group_at + p] = gathered(ext, p) + vb[WIDE + p] + control[step] * dipole
        src = pot.at[step, pl.ds(group_at + 2 * core, 2)]
        return [push(src, src, o, RING * g + mate(k)) for k in range(1, RING)]

    def swap_potential(step):
        pieces = [pot.at[step, pl.ds(WIDE + SLAB * mate(k) + 2 * core, 2)] for k in range(1, RING)]
        return [push(piece, piece, sibling, d) for piece in pieces]

    def spread_halo(step):
        at = pot.at[step]
        return [
            push(at.at[pl.ds(WIDE + GROUP - 6 + 3 * core, 3)], at.at[pl.ds(WIDE - 6 + 3 * core, 3)], o, after_group),
            push(at.at[pl.ds(WIDE + 3 * core, 3)], at.at[pl.ds(WIDE + GROUP + 3 * core, 3)], o, before_group),
        ]

    def swap_halo(step):
        at = pot.at[step]
        pieces = [at.at[pl.ds(WIDE - 6 + 3 * core, 3)], at.at[pl.ds(WIDE + GROUP + 3 * core, 3)]]
        return [push(piece, piece, sibling, d) for piece in pieces]

    def halo(step, begin, count):
        ref = psi.at[step]
        far = begin + count
        return [
            push(
                ref.at[:, pl.ds(WIDE + GROUP - far, count)],
                ref.at[:, pl.ds(WIDE - far, count)],
                o,
                after_group,
            ),
            push(
                ref.at[:, pl.ds(WIDE + begin, count)],
                ref.at[:, pl.ds(WIDE + GROUP + begin, count)],
                o,
                before_group,
            ),
        ]

    def image(src, c, p, full):
        u = src[c, p]
        y_near, y_far = y_pairs(u, 2)
        near = (src[c, p - 1] + src[c, p + 1]) + (y_near + z_pair(u, 1))
        far = (src[c, p - 2] + src[c, p + 2]) + (y_far + z_pair(u, 2))
        return full * u - (2.0 / 3.0) * near + (1.0 / 24.0) * far

    def group_range(lo, hi, body):
        begin = jnp.maximum(lo, WIDE - GROUP * g)
        end = jnp.minimum(hi, WIDE + NX - GROUP * g)

        def run(p, carry):
            body(begin + 2 * p)
            body(begin + 2 * p + 1)
            return carry

        lax.fori_loop(0, (end - begin) // 2, run, 0)

    def term(step, order, lo, hi):
        src, dst = ((psi.at[step], t1), (t1, t2), (t2, t3), (t3, None))[order - 1]
        factor = TIME_STEP / order

        def body(p):
            full = pot[step, p] + 3.75
            re = factor * image(src, 1, p, full)
            im = -factor * image(src, 0, p, full)
            if order < TERMS:
                dst[0, p] = re
                dst[1, p] = im
                return
            re = re + (psi[step, 0, p] + t1[0, p]) + (t2[0, p] + t3[0, p])
            im = im + (psi[step, 1, p] + t1[1, p]) + (t2[1, p] + t3[1, p])
            if step == STEPS - 1:
                scatter(psi, re, step + 1, 0, p)
                scatter(psi, im, step + 1, 1, p)
            else:
                psi[step + 1, 0, p] = re
                psi[step + 1, 1, p] = im
                ringpart[p - WIDE] = weight(x) * (re * re + im * im)

        group_range(lo, hi, body)

    def inside(step):
        for order in range(1, TERMS + 1):
            cut = 2 * (order - 1)
            term(step, order, WIDE + cut, WIDE + GROUP - cut)

    def low_edge(step):
        for order in range(1, TERMS + 1):
            term(step, order, 2 * order, 2 * order + 6)

    def high_edge(step):
        for order in range(1, TERMS + 1):
            term(step, order, EXT - 6 - 2 * order, EXT - 2 * order)

    class Shares:
        def __init__(self, src_of, dst_of):
            self.copies = []
            for k in range(1, RING):
                to = mate(k)
                i = len(pending)
                copy = pltpu.make_async_remote_copy(
                    src_ref=src_of(to),
                    dst_ref=dst_of(k),
                    send_sem=send.at[i],
                    recv_sem=recv.at[i],
                    device_id={"orb": o, "dom": RING * g + to},
                    device_id_type=pl.DeviceIdType.MESH,
                )
                pending.append(copy)
                self.copies.append((to, copy))

        def begin(self, lo, hi):
            for to, copy in self.copies:
                pl.when(jnp.logical_and(to >= lo, to < hi))(copy.start)

        def wait(self):
            for unused, copy in self.copies:
                copy.wait_recv()

    regroup = []

    def begin_regroup():
        for k in range(1, RING):
            to = mate(k)
            regroup.append(
                push(psi_in.at[:, to], land.at[:, pl.ds(SLAB * x, SLAB)], o, RING * g + to)
            )

    halos = {}

    def regrouped():
        for copy in regroup:
            copy.wait_recv()
        own.wait()

        def reorder(p, carry):
            for c in range(2):
                psi[0, c, WIDE + p] = gathered(land, c, p)
            return carry

        lax.fori_loop(0, GROUP, reorder, 0)

    plans = (
        {"near": ("begin",), "source": ("end", (0, 2)), "again": ((2, 3),), "solved": ((5, 3),)},
        {"source": ((0, 2),), "again": ((2, 3),), "solved": ((5, 3),)},
    )

    def meanwhile(step, place):
        for what in plans[step].get(place, ()):
            if what == "begin":
                begin_regroup()
            elif what == "end":
                regrouped()
            else:
                halos[what] = halo(step, *what)

    def clear_outside(step, begin, count):
        @pl.when(g == 0)
        def _():
            clear_halo(WIDE - begin - count, count, (psi.at[step],))

        @pl.when(g == GROUPS - 1)
        def _():
            clear_halo(WIDE + GROUP + begin, count, (psi.at[step],))

    for step in range(STEPS):
        meanwhile(step, "start")
        solve(step, functools.partial(meanwhile, step))
        meanwhile(step, "solved")
        spread = spread_potential(step)
        meanwhile(step, "spread")
        for copy in spread:
            copy.wait_recv()
        for copy in swap_potential(step):
            copy.wait_recv()
        spread = spread_halo(step)
        meanwhile(step, "beside")
        ready = [halos.pop(key) for key in sorted(halos)]
        for copy in ready[0]:
            copy.wait_recv()
        clear_outside(step, 0, 2)
        inside(step)
        for copy in sum(ready[1:], []):
            copy.wait_recv()
        clear_outside(step, 2, 6)
        for copy in spread:
            copy.wait_recv()
        for copy in swap_halo(step):
            copy.wait_recv()
        later = psi.at[step + 1]
        if step < STEPS - 1:
            shares = Shares(
                lambda to: ringpart.at[pl.ds(SLAB * to, SLAB)],
                lambda k: ringpart.at[pl.ds(GROUP + SLAB * (k - 1), SLAB)],
            )
        else:
            shares = Shares(
                lambda to: later.at[:, pl.ds(WIDE + SLAB * to, SLAB)],
                lambda k: psi_out.at[:, x],
            )
        low_edge(step)
        shares.begin(0, RING // 2)
        high_edge(step)
        shares.begin(RING // 2, RING)
        if step < STEPS - 1:
            shares.wait()
            for p in range(SLAB):
                total = ringpart[SLAB * x + p]
                for k in range(1, RING):
                    total = total + ringpart[GROUP + SLAB * (k - 1) + p]
                part[step + 1, p] = total

    for p in range(SLAB):
        scatter(hartree_out, vb[WIDE + p], p)
    final = psi.at[STEPS]
    own = pltpu.make_async_copy(
        final.at[:, pl.ds(group_at, SLAB)], psi_out.at[:, x], local_sem.at[1]
    )
    own.start()
    shares.wait()
    own.wait()
    for copy in pending:
        copy.wait_send()


def per_device(orbitals, occupations, external, control):
    f32 = jnp.float32
    vmem = pl.BlockSpec(memory_space=pltpu.VMEM)
    smem = pl.BlockSpec(memory_space=pltpu.SMEM)
    fields = pltpu.VMEM((2, EXT, NY, NZ), f32)
    slab = pltpu.VMEM((STEPS, SLAB, NY, NZ), f32)
    slab_one = pltpu.VMEM((SLAB, NY, NZ), f32)
    mid = pltpu.VMEM((SLABS + 2, Y1, NZ), f32)
    low = pltpu.VMEM((SLABS + 2, Y2, NZ), f32)
    return pl.pallas_call(
        kernel,
        out_shape=(
            jax.ShapeDtypeStruct(orbitals.shape, f32),
            jax.ShapeDtypeStruct(external.shape, f32),
        ),
        in_specs=[vmem, smem, vmem, smem],
        out_specs=(pl.BlockSpec(memory_space=pl.ANY), vmem),
        scratch_shapes=[
            pltpu.VMEM((STEPS + 1, 2, EXT, NY, NZ), f32),
            fields, fields, fields,
            pltpu.VMEM((STEPS, EXT, NY, NZ), f32),
            slab,
            pltpu.VMEM((GROUP + SLAB * (RING - 1), NY, NZ), f32),
            slab, slab, slab,
            pltpu.VMEM((STEPS, FEXT, NY, NZ), f32),
            pltpu.VMEM((FEXT, NY, NZ), f32),
            pltpu.VMEM((FEXT, NY, NZ), f32),
            pltpu.VMEM((STEPS, 2, SLABS, 2, Y2, NZ), f32),
            mid, mid, low, low,
            pltpu.VMEM((SLABS, Y1, NZ), f32),
            pltpu.VMEM((SLABS, Y2, NZ), f32),
            pltpu.VMEM((2, GROUP, NY, NZ), f32),
            slab_one,
            pltpu.VMEM((SLABS, Y2, NZ), f32),
            pltpu.VMEM((10, NY, NZ), f32),
            pltpu.SemaphoreType.DMA((COPIES,)),
            pltpu.SemaphoreType.DMA((COPIES,)),
            pltpu.SemaphoreType.DMA((2,)),
        ],
        compiler_params=pltpu.CompilerParams(
            collective_id=0, has_side_effects=True, vmem_limit_bytes=56 * 1024 * 1024
        ),
    )(orbitals, occupations, external, control)


def solution(mesh):
    in_specs = (P(None, "orb", "dom", None, None), P("orb"), P("dom", None, None), P())
    out_specs = (P(None, "orb", "dom", None, None), P("dom", None, None))
    return jax.shard_map(
        per_device, mesh=mesh, in_specs=in_specs, out_specs=out_specs, check_vma=False
    )
```
